128 devices in a mesh: ctx: 8 (over y, x_lo), grp: 16 (over z, x_hi, core).
Axes of the slice: x: 4 (x_hi: 2, x_lo: 2; x = x_hi * 2 + x_lo), y: 4, z: 4, core: 2. Of those that a mesh axis runs over, the one named last changes fastest.
Arguments:
- features: bfloat16 [3, 4096, 8192], P(None, 'ctx', 'grp'), may hold values from -6 to 6
- short_weight: float32 [3, 3, 8192], P(None, None, 'grp'), may hold values from -3 to 3
- long_filter: bfloat16 [4096, 8192], P('ctx', 'grp'), may hold values from -0.1875 to 0.1875
- lengths: int32 [32], replicated, may hold values from 128 to 4096, as said below
- skip_gain: float32 [8192], P('grp'), may hold values from 0.5 to 1.5
- out_weight: bfloat16 [8192, 8192], P('grp'), may hold values from -0.0625 to 0.0625
Outputs:
- mixed: bfloat16 [4096, 8192], P('ctx', 'grp')
The draws below stay inside these ranges and needn't reach their ends.
Inputs may be any that keep to these rules, and one draw needn't show every extreme that they name: `lengths`: every length is a multiple of 128; some group has length 4096 and some group has length 128.
All inputs are finite; a program needn't handle non-finite values.
Results may differ from the reference program's by a relative error of at most 0.0049.
Values may be sent and summed in bfloat16 or wider, within the bound.
A program may use at most 192 MiB of HBM per device.

```python
import jax
import jax.numpy as jnp
from jax import lax

D = 8192
GROUP_CH = 256
STEP = 128
TOKENS = 4096
GROUPS = 32


def draw_lengths(key, part):
    key = jax.random.fold_in(key, 5)
    first, second = jax.random.split(key)
    counts = jax.random.randint(first, (GROUPS,), 1, TOKENS // STEP + 1)
    order = jax.random.permutation(second, GROUPS)
    counts = counts.at[order[0]].set(TOKENS // STEP).at[order[1]].set(1)
    return (counts * STEP).astype(jnp.int32)


def steps_of(stream_key, dims, cuts, least, high):
    def one(axis_at, blocks):
        steps = jax.random.uniform(jax.random.fold_in(jax.random.fold_in(stream_key, 6), axis_at), (blocks,), jnp.float32, least / len(cuts), high / len(cuts))
        return jnp.repeat(jnp.exp(steps), dims[axis_at] // blocks).reshape((-1,) + (1,) * (len(dims) - axis_at - 1))

    gain = one(*cuts[0])
    for cut in cuts[1:]:
        gain = gain * one(*cut)
    return gain


def centred(key, extent, scale, limit, cuts=(), kind=jnp.bfloat16):
    array = jax.random.normal(key, extent, jnp.float32) * scale
    if len(cuts) > 0:
        array = steps_of(key, extent, cuts, -0.22, 0.18) * array
    return jnp.clip(array, min=-limit, max=limit).astype(kind)


def setup_inputs(seed: int = 0) -> dict:
    seeds = jax.random.split(jax.random.key(seed), 7)
    features = centred(seeds[0], (3, TOKENS, D), 1.0, 6.0, ((1, 8), (2, 16)))
    short_weight = centred(seeds[1], (3, 3, D), 0.6, 3.0, ((2, 16),), jnp.float32)
    long_filter = centred(seeds[2], (TOKENS, D), (TOKENS // 4) ** -0.5, 0.1875, ((0, 8), (1, 16)))
    lengths = draw_lengths(jax.random.fold_in(seeds[6], 71), 0)
    skip_gain = jnp.clip(0.5 + 1.0 * jax.random.uniform(seeds[4], (D,), jnp.float32) ** steps_of(seeds[4], (D,), ((0, 16),), -0.2, 0.2), 0.5, 1.5)
    out_weight = centred(seeds[5], (D, D), D ** -0.5, 0.0625, ((0, 16),))
    return {"features": features, "short_weight": short_weight, "long_filter": long_filter, "lengths": lengths, "skip_gain": skip_gain, "out_weight": out_weight}


def reference(features, short_weight, long_filter, lengths, skip_gain, out_weight):
    feats = features.astype(jnp.float32)
    padded = jnp.pad(feats, ((0, 0), (2, 0), (0, 0)))
    short = short_weight[0][:, None, :] * padded[:, 2:, :]
    short = short + short_weight[1][:, None, :] * padded[:, 1:-1, :]
    short = short + short_weight[2][:, None, :] * padded[:, :-2, :]
    query = short[0]
    signal = short[1] * short[2]
    chan_len = jnp.repeat(lengths, GROUP_CH)
    lags = jnp.arange(TOKENS, dtype=jnp.int32)
    cut = jnp.where(lags[:, None] < chan_len[None, :], long_filter.astype(jnp.float32), jnp.float32(0.0))
    sig_blocks = signal.reshape(TOKENS, GROUPS, GROUP_CH).transpose(1, 0, 2)
    cut_blocks = cut.reshape(TOKENS, GROUPS, GROUP_CH).transpose(1, 0, 2)

    def convolve(pair):
        sig, fil = pair
        spec = jnp.fft.rfft(sig, n=2 * TOKENS, axis=0) * jnp.fft.rfft(fil, n=2 * TOKENS, axis=0)
        return jnp.fft.irfft(spec, n=2 * TOKENS, axis=0)[:TOKENS]

    conv = lax.map(convolve, (sig_blocks, cut_blocks))
    conv = conv.transpose(1, 0, 2).reshape(TOKENS, D)
    gated = (query * (conv + skip_gain[None, :] * signal)).astype(jnp.bfloat16)
    return jnp.dot(gated, out_weight, preferred_element_type=jnp.float32).astype(jnp.bfloat16)
```

```python
import numpy as np

import jax
import jax.numpy as jnp
import ml_dtypes
from jax import lax
from jax.experimental import pallas as pl
from jax.experimental.pallas import tpu as pltpu
from jax.sharding import PartitionSpec as P

GROUP_CH = 256
SPAN = 512
WIDTH = 512
NCTX = 8
OWN = WIDTH // NCTX
HALF = SPAN // 2
QUART = SPAN // 4
BF = jnp.bfloat16
F32 = jnp.float32
MESH = pl.DeviceIdType.MESH


def tables():
    freq = np.concatenate([np.arange(0, SPAN, 2), np.arange(1, SPAN, 2)])
    angle = np.pi * ((np.arange(SPAN)[:, None] * (2 * freq + 1)[None, :]) % (4 * SPAN)) / (2 * SPAN)
    forward = np.concatenate([np.cos(angle), -np.sin(angle)], axis=1)
    high = forward.astype(ml_dtypes.bfloat16)
    low = (forward - high.astype(np.float64)).astype(ml_dtypes.bfloat16)
    scale = ml_dtypes.bfloat16(1.0 / SPAN)
    return (
        np.stack([high, low]),
        np.stack([np.ascontiguousarray(high.T) * scale, np.ascontiguousarray(low.T) * scale]),
    )


def nt(lhs, rhs):
    return lax.dot_general(lhs, rhs, (((1,), (1,)), ((), ())), preferred_element_type=F32)


def mm(lhs, rhs):
    return jnp.dot(lhs, rhs, preferred_element_type=F32)


def kernel(
    lens, sw, skip, feat, filt, weight, fwd_hbm, inv_hbm,
    out,
    ext, halo, ftmp, fsend, frecv, sbf, ssend, srecv, qbuf, sbuf, fwd, inv, eye,
    spec_h, spec_x, spec_y, yhi, ylo, csend, crecv, gbuf, wbuf,
    xsend, xrecv, z1send, z1recv, z2send, z2recv, zxsend, zxrecv,
    s1send, s1recv, s2send, s2recv, keep,
    loc, wloc, hs, hr, fs, fr, ss, sr, ws, wr, cs, cr, gs, gr,
    xs, xr, z1s, z1r, z2s, z2r, zxs, zxr, s1s, s1r, s2s, s2r,
):
    c, g = lax.axis_index("ctx"), lax.axis_index("grp")
    z, xh, core = g // 4, (g // 2) % 2, g % 2
    partner = (c, g + 1 - 2 * core)
    across = (c, g + 2 - 4 * xh)
    up = (c, ((z + 1) % 4) * 4 + xh * 2 + core)
    down = (c, ((z + 3) % 4) * 4 + xh * 2 + core)

    def remote(src, dst, send, recv, device):
        return pltpu.make_async_remote_copy(
            src_ref=src, dst_ref=dst, send_sem=send, recv_sem=recv, device_id=device, device_id_type=MESH
        )

    sent = []

    def start(*args):
        copy = remote(*args)
        copy.start()
        sent.append(copy)

    def arrived(dst, recv):
        remote(dst, dst, hs.at[0], recv, partner).wait_recv()

    def rows64(ref, index):
        return ref.at[pl.ds(pl.multiple_of(index * OWN, OWN), OWN)]

    get_filt = pltpu.make_async_copy(filt, ftmp, loc.at[0])
    get_feat = pltpu.make_async_copy(feat, ext.at[:, pl.ds(16, SPAN)], loc.at[1])
    get_fwd = pltpu.make_async_copy(fwd_hbm, fwd, loc.at[2])
    get_inv = pltpu.make_async_copy(inv_hbm, inv, loc.at[3])
    get_filt.start()
    get_feat.start()
    get_fwd.start()
    get_inv.start()
    mine = pl.ds(pl.multiple_of(core * WIDTH, WIDTH), WIDTH)

    barrier = pltpu.get_barrier_semaphore()
    peers = [(lax.rem(c + k, NCTX), g) for k in range(1, NCTX)]
    for device in peers + [partner, across, up, down]:
        pl.semaphore_signal(barrier, inc=1, device_id=device, device_id_type=MESH)

    eye[...] = (
        lax.broadcasted_iota(jnp.int32, (HALF, HALF), 0) == lax.broadcasted_iota(jnp.int32, (HALF, HALF), 1)
    ).astype(F32).astype(BF)
    get_filt.wait()
    for part in range(WIDTH // GROUP_CH):
        length = lens[2 * g + part]
        cols = pl.ds(part * GROUP_CH, GROUP_CH)
        lag = c * SPAN + lax.broadcasted_iota(jnp.int32, (SPAN, GROUP_CH), 0)
        cut = jnp.where(lag < length, ftmp[:, cols].astype(F32), 0.0).astype(BF)
        fsend[cols, :] = nt(eye[...], cut).astype(BF)

    pl.semaphore_wait(barrier, len(peers) + 4)
    start(feat.at[:, pl.ds(SPAN - 16, 16)], halo, hs.at[0], hr.at[0], peers[0])
    for k, peer in enumerate(peers):
        start(rows64(fsend, peer[0]), rows64(frecv, c), fs.at[k], fr.at[c], peer)
    own_f = pltpu.make_async_copy(rows64(fsend, c), rows64(frecv, c), fr.at[c])
    own_f.start()

    get_feat.wait()

    def short(block):
        base = pl.multiple_of(block * 32, 32)
        here = pl.ds(base, 32)
        res = []
        for i in range(3):
            v = ext[i, pl.ds(base, 48), :].astype(F32)
            acc = sw[0, i : i + 1, :] * v[16:]
            acc = acc + sw[1, i : i + 1, :] * pltpu.roll(v, 1, 0)[16:]
            acc = acc + sw[2, i : i + 1, :] * pltpu.roll(v, 2, 0)[16:]
            res.append(acc)
        qbuf[here, :] = res[0]
        signal = res[1] * res[2]
        sbuf[here, :] = signal
        sbf[here, :] = signal.astype(BF)

    @pl.loop(1, SPAN // 32)
    def _(block):
        short(block)

    arrived(halo, hr.at[0])
    first = lax.broadcast_in_dim(c, (3, 16, WIDTH), ()) > 0
    ext[:, pl.ds(0, 16), :] = jnp.where(first, halo[...].astype(F32), 0.0).astype(BF)
    short(0)
    for part in range(2):
        cols = pl.ds(part * HALF, HALF)
        ssend[cols, :] = nt(eye[...], sbf[:, cols]).astype(BF)
    for k, peer in enumerate(peers):
        start(rows64(ssend, peer[0]), rows64(srecv, c), ss.at[k], sr.at[c], peer)
    own_s = pltpu.make_async_copy(rows64(ssend, c), rows64(srecv, c), sr.at[c])
    own_s.start()

    get_w = []
    for p in range(8):
        keep_cols = pl.ds(pl.multiple_of((2 * p + core) * WIDTH, WIDTH), WIDTH)
        give_cols = pl.ds(pl.multiple_of((2 * p + 1 - core) * WIDTH, WIDTH), WIDTH)
        copy = pltpu.make_async_copy(weight.at[:, keep_cols], wbuf.at[p, mine], wloc.at[p])
        copy.start()
        get_w.append(copy)
        start(weight.at[:, give_cols], wbuf.at[p, mine], ws.at[p], wr.at[p], partner)

    get_fwd.wait()

    def transform(block, spec):
        @pl.loop(0, 4)
        def _(n):
            cols = pl.ds(pl.multiple_of(n * HALF, HALF), HALF)
            spec[:, cols] = mm(block[...], fwd[0, :, cols]) + mm(block[...], fwd[1, :, cols])

    for k in range(NCTX):
        arrived(rows64(frecv, k), fr.at[k])
    transform(frecv, spec_h)
    for k in range(NCTX):
        arrived(rows64(srecv, k), sr.at[k])
    transform(srecv, spec_x)

    for lane in range(4):
        re, im = pl.ds(lane * 128, 128), pl.ds(SPAN + lane * 128, 128)

        @pl.loop(0, OWN // 8)
        def _(r, re=re, im=im, odd=lane >= 2):
            def at(spec, block, cols):
                return spec[pl.ds(pl.multiple_of(block * OWN + r * 8, 8), 8), cols]

            h_re = [at(spec_h, d, re) for d in range(NCTX)]
            h_im = [at(spec_h, d, im) for d in range(NCTX)]
            if odd:
                g_re = [h_re[0]] + [h_re[d] + h_im[d - 1] for d in range(1, NCTX)]
                g_im = [h_im[0]] + [h_im[d] - h_re[d - 1] for d in range(1, NCTX)]
            else:
                g_re = [h_re[0]] + [h_re[d] - h_im[d - 1] for d in range(1, NCTX)]
                g_im = [h_im[0]] + [h_im[d] + h_re[d - 1] for d in range(1, NCTX)]
            x_re = [at(spec_x, j, re) for j in range(NCTX)]
            x_im = [at(spec_x, j, im) for j in range(NCTX)]
            for i in range(NCTX):
                y_re = x_re[0] * g_re[i] - x_im[0] * g_im[i]
                y_im = x_re[0] * g_im[i] + x_im[0] * g_re[i]
                for j in range(1, i + 1):
                    y_re = y_re + x_re[j] * g_re[i - j] - x_im[j] * g_im[i - j]
                    y_im = y_im + x_re[j] * g_im[i - j] + x_im[j] * g_re[i - j]
                rows = pl.ds(pl.multiple_of(i * OWN + r * 8, 8), 8)
                spec_y[rows, re] = y_re
                spec_y[rows, im] = y_im

    @pl.loop(0, 16)
    def _(r):
        rows = pl.ds(pl.multiple_of(r * 32, 32), 32)
        value = spec_y[rows, :]
        high = value.astype(BF)
        yhi[rows, :] = high
        ylo[rows, :] = (value - high.astype(F32)).astype(BF)

    get_inv.wait()
    for h in range(2):
        cols = pl.ds(h * HALF, HALF)
        back = mm(yhi[...], inv[0, :, cols]) + mm(ylo[...], inv[0, :, cols]) + mm(yhi[...], inv[1, :, cols])
        csend[h] = back.astype(BF)
        for k, peer in enumerate(peers):
            start(
                rows64(csend.at[h], peer[0]), rows64(crecv.at[h], c), cs.at[h, k], cr.at[h, c], peer
            )
        pltpu.make_async_copy(rows64(csend.at[h], c), rows64(crecv.at[h], c), cr.at[h, c]).start()

    def gate(h):
        for k in range(NCTX):
            arrived(rows64(crecv.at[h], k), cr.at[h, k])
        rows = pl.ds(h * HALF, HALF)
        conv = nt(eye[...], crecv[h])
        gated = qbuf[rows, :] * (conv + skip[...] * sbuf[rows, :])
        gbuf[h, core] = gated.astype(BF)
        start(gbuf.at[h, core], gbuf.at[h, core], gs.at[h], gr.at[h], partner)

    def met(h):
        arrived(gbuf.at[h, 1 - core], gr.at[h])

    def project(h, dz, other):
        p = ((z + dz) % 4) * 2 + (xh if other == 0 else 1 - xh)
        return mm(gbuf[h, 0], wbuf[p, :WIDTH, :]) + mm(gbuf[h, 1], wbuf[p, WIDTH:, :])

    top, low = pl.ds(0, QUART), pl.ds(QUART, QUART)

    gate(0)
    gate(1)
    for p in range(8):
        get_w[p].wait()
        arrived(wbuf.at[p, pl.ds(pl.multiple_of((1 - core) * WIDTH, WIDTH), WIDTH)], wr.at[p])
    met(0)
    for dz in (2, 1, 3, 0):
        xsend[dz] = project(0, dz, 1).astype(BF)
        start(xsend.at[dz], xrecv.at[dz], xs.at[dz], xr.at[dz], across)
    met(1)
    for o in range(2):
        z1send[o] = project(1, 2, o).astype(BF)
        start(z1send.at[o, top], z1recv.at[0, o], z1s.at[0, o], z1r.at[0, o], up)
        start(z1send.at[o, low], z1recv.at[1, o], z1s.at[1, o], z1r.at[1, o], down)
    for d, dz, rows, device in ((0, 1, top, up), (1, 3, low, down)):
        for o in range(2):
            z2send[d, o] = project(1, dz, o).astype(BF)
            arrived(z1recv.at[d, o], z1r.at[d, o])
            z2send[d, o, rows] = (z2send[d, o, rows].astype(F32) + z1recv[d, o].astype(F32)).astype(BF)
            start(z2send.at[d, o], z2recv.at[d, o], z2s.at[d, o], z2r.at[d, o], device)

    def summed(dz):
        keep[...] = project(0, dz, 0)
        arrived(xrecv.at[dz], xr.at[dz])
        keep[...] += xrecv[dz].astype(F32)

    summed(2)
    s1send[...] = keep[...].astype(BF)
    start(s1send.at[top], s1recv.at[0], s1s.at[0], s1r.at[0], up)
    start(s1send.at[low], s1recv.at[1], s1s.at[1], s1r.at[1], down)
    for d, dz, rows, device in ((0, 1, top, up), (1, 3, low, down)):
        summed(dz)
        arrived(s1recv.at[d], s1r.at[d])
        keep[rows, :] += s1recv[d].astype(F32)
        s2send[d] = keep[...].astype(BF)
        start(s2send.at[d], s2recv.at[d], s2s.at[d], s2r.at[d], device)

    def gathered(o):
        keep[...] = project(1, 0, o)
        for d in range(2):
            arrived(z2recv.at[d, o], z2r.at[d, o])
        keep[...] += z2recv[0, o].astype(F32) + z2recv[1, o].astype(F32)

    gathered(1)
    zxsend[...] = keep[...].astype(BF)
    start(zxsend, zxrecv, zxs.at[0], zxr.at[0], across)
    summed(0)
    for d in range(2):
        arrived(s2recv.at[d], s2r.at[d])
    out[pl.ds(0, HALF), :] = (keep[...] + s2recv[0].astype(F32) + s2recv[1].astype(F32)).astype(BF)
    gathered(0)
    arrived(zxrecv, zxr.at[0])
    out[pl.ds(HALF, HALF), :] = (keep[...] + zxrecv[...].astype(F32)).astype(BF)
    for copy in sent:
        copy.wait_send()


def per_device(features, short_weight, long_filter, lengths, skip_gain, out_weight):
    forward, inverse = tables()
    dma = pltpu.SemaphoreType.DMA
    vm = pltpu.VMEM
    block = (HALF, WIDTH)
    scratch = [
        vm((3, 16 + SPAN, WIDTH), BF), vm((3, 16, WIDTH), BF),
        vm((SPAN, WIDTH), BF), vm((WIDTH, SPAN), BF), vm((WIDTH, SPAN), BF),
        vm((SPAN, WIDTH), BF), vm((WIDTH, SPAN), BF), vm((WIDTH, SPAN), BF),
        vm((SPAN, WIDTH), F32), vm((SPAN, WIDTH), F32),
        vm((2, SPAN, 2 * SPAN), BF), vm((2, 2 * SPAN, SPAN), BF), vm((HALF, HALF), BF),
        vm((WIDTH, 2 * SPAN), F32), vm((WIDTH, 2 * SPAN), F32), vm((WIDTH, 2 * SPAN), F32),
        vm((WIDTH, 2 * SPAN), BF), vm((WIDTH, 2 * SPAN), BF),
        vm((2, WIDTH, HALF), BF), vm((2, WIDTH, HALF), BF),
        vm((2, 2) + block, BF), vm((8, 2 * WIDTH, WIDTH), BF),
        vm((4,) + block, BF), vm((4,) + block, BF),
        vm((2,) + block, BF), vm((2, 2, QUART, WIDTH), BF),
        vm((2, 2) + block, BF), vm((2, 2) + block, BF),
        vm(block, BF), vm(block, BF),
        vm(block, BF), vm((2, QUART, WIDTH), BF),
        vm((2,) + block, BF), vm((2,) + block, BF), vm(block, F32),
        dma((4,)), dma((8,)), dma((1,)), dma((1,)),
        dma((7,)), dma((8,)), dma((7,)), dma((8,)), dma((8,)), dma((8,)),
        dma((2, 7)), dma((2, 8)), dma((2,)), dma((2,)),
        dma((4,)), dma((4,)), dma((2, 2)), dma((2, 2)), dma((2, 2)), dma((2, 2)),
        dma((1,)), dma((1,)), dma((2,)), dma((2,)), dma((2,)), dma((2,)),
    ]
    hbm = pl.BlockSpec(memory_space=pl.ANY)
    near = pl.BlockSpec(memory_space=pltpu.VMEM)
    return pl.pallas_call(
        kernel,
        out_shape=jax.ShapeDtypeStruct((SPAN, WIDTH), BF),
        in_specs=[pl.BlockSpec(memory_space=pltpu.SMEM), near, near, hbm, hbm, hbm, hbm, hbm],
        out_specs=near,
        scratch_shapes=scratch,
        name="hyena",
        compiler_params=pltpu.CompilerParams(
            collective_id=0, has_side_effects=True, vmem_limit_bytes=56 * 2**20
        ),
    )(
        lengths, short_weight, skip_gain.reshape(1, WIDTH), features, long_filter, out_weight,
        jnp.asarray(forward), jnp.asarray(inverse),
    )


def solution(mesh):
    return jax.shard_map(
        per_device,
        mesh=mesh,
        in_specs=(
            P(None, "ctx", "grp"),
            P(None, None, "grp"),
            P("ctx", "grp"),
            P(),
            P("grp"),
            P("grp", None),
        ),
        out_specs=P("ctx", "grp"),
        check_vma=False,
    )
```

```python
import numpy as np

import jax
import jax.numpy as jnp
import ml_dtypes
from jax import lax
from jax.experimental import pallas as pl
from jax.experimental.pallas import tpu as pltpu
from jax.sharding import PartitionSpec as P

GROUP_CH = 256
SPAN = 512
WIDTH = 512
NCTX = 8
OWN = WIDTH // NCTX
BATCH = OWN // 2
HALF = SPAN // 2
QUART = SPAN // 4
BF = jnp.bfloat16
F32 = jnp.float32
MESH = pl.DeviceIdType.MESH


def tables():
    freq = np.concatenate([np.arange(0, SPAN, 2), np.arange(1, SPAN, 2)])
    angle = np.pi * ((np.arange(SPAN)[:, None] * (2 * freq + 1)[None, :]) % (4 * SPAN)) / (2 * SPAN)
    forward = np.concatenate([np.cos(angle), -np.sin(angle)], axis=1)
    high = forward.astype(ml_dtypes.bfloat16)
    low = (forward - high.astype(np.float64)).astype(ml_dtypes.bfloat16)
    scale = ml_dtypes.bfloat16(1.0 / SPAN)
    return (
        np.stack([high, low]),
        np.stack([np.ascontiguousarray(high.T) * scale, np.ascontiguousarray(low.T) * scale]),
    )


def nt(lhs, rhs):
    return lax.dot_general(lhs, rhs, (((1,), (1,)), ((), ())), preferred_element_type=F32)


def mm(lhs, rhs):
    return jnp.dot(lhs, rhs, preferred_element_type=F32)


def kernel(
    lens, sw, skip, feat, filt, weight, fwd_hbm, inv_hbm,
    out,
    ext, edge, halo, ftmp, fsend, frecv, sbf, ssend, srecv, qbuf, sbuf, fwd, inv, eye,
    spec_h, spec_x, spec_y, yhi, ylo, csend, crecv, gbuf, wbuf,
    xsend, xrecv, z1send, z1recv, z2send, z2recv, zxsend, zxrecv,
    s1send, s1recv, s2send, s2recv, keep,
    loc, wloc, hs, hr, fs, fr, ss, sr, ws, wr, cs, cr, gs, gr,
    xs, xr, z1s, z1r, z2s, z2r, zxs, zxr, s1s, s1r, s2s, s2r,
):
    c, g = lax.axis_index("ctx"), lax.axis_index("grp")
    z, xh, core = g // 4, (g // 2) % 2, g % 2
    partner = (c, g + 1 - 2 * core)
    across = (c, g + 2 - 4 * xh)
    up = (c, ((z + 1) % 4) * 4 + xh * 2 + core)
    down = (c, ((z + 3) % 4) * 4 + xh * 2 + core)

    def remote(src, dst, send, recv, device):
        return pltpu.make_async_remote_copy(
            src_ref=src, dst_ref=dst, send_sem=send, recv_sem=recv, device_id=device, device_id_type=MESH
        )

    sent = []

    def start(*args):
        copy = remote(*args)
        copy.start()
        sent.append(copy)

    def arrived(dst, recv):
        remote(dst, dst, hs.at[0], recv, partner).wait_recv()

    def rows64(ref, index):
        return ref.at[pl.ds(pl.multiple_of(index * OWN, OWN), OWN)]

    def rows32(ref, index):
        return ref.at[pl.ds(pl.multiple_of(index * BATCH, BATCH), BATCH)]

    get_filt = pltpu.make_async_copy(filt, ftmp, loc.at[0])
    get_feat = pltpu.make_async_copy(feat, ext.at[:, pl.ds(16, SPAN)], loc.at[1])
    get_fwd = pltpu.make_async_copy(fwd_hbm, fwd, loc.at[2])
    get_inv = pltpu.make_async_copy(inv_hbm, inv, loc.at[3])
    get_filt.start()
    get_feat.start()
    get_fwd.start()
    get_inv.start()
    mine = pl.ds(pl.multiple_of(core * WIDTH, WIDTH), WIDTH)

    barrier = pltpu.get_barrier_semaphore()
    peers = [(lax.rem(c + k, NCTX), g) for k in range(1, NCTX)]
    for device in peers + [partner, across, up, down]:
        pl.semaphore_signal(barrier, inc=1, device_id=device, device_id_type=MESH)

    eye[...] = (
        lax.broadcasted_iota(jnp.int32, (HALF, HALF), 0) == lax.broadcasted_iota(jnp.int32, (HALF, HALF), 1)
    ).astype(F32).astype(BF)
    get_filt.wait()
    for part in range(WIDTH // GROUP_CH):
        length = lens[2 * g + part]
        cols = pl.ds(part * GROUP_CH, GROUP_CH)
        lag = c * SPAN + lax.broadcasted_iota(jnp.int32, (SPAN, GROUP_CH), 0)
        cut = jnp.where(lag < length, ftmp[:, cols].astype(F32), 0.0).astype(BF)
        fsend[cols, :] = nt(eye[...], cut).astype(BF)

    get_feat.wait()
    row = lax.broadcasted_iota(jnp.int32, (16, WIDTH), 0)
    packed = jnp.zeros((16, WIDTH), F32)
    for i in range(3):
        last = pltpu.roll(ext[i, pl.ds(SPAN, 16), :].astype(F32), 2 + 2 * i, 0)
        packed = jnp.where(row // 2 == i, last, packed)
    edge[...] = packed.astype(BF)

    pl.semaphore_wait(barrier, len(peers) + 4)
    start(edge, halo, hs.at[0], hr.at[0], peers[0])
    for k, peer in enumerate(peers):
        start(rows64(fsend, peer[0]), rows64(frecv, c), fs.at[k], fr.at[c], peer)
    own_f = pltpu.make_async_copy(rows64(fsend, c), rows64(frecv, c), fr.at[c])
    own_f.start()


    def short(block):
        base = pl.multiple_of(block * 32, 32)
        here = pl.ds(base, 32)
        res = []
        for i in range(3):
            v = ext[i, pl.ds(base, 48), :].astype(F32)
            acc = sw[0, i : i + 1, :] * v[16:]
            acc = acc + sw[1, i : i + 1, :] * pltpu.roll(v, 1, 0)[16:]
            acc = acc + sw[2, i : i + 1, :] * pltpu.roll(v, 2, 0)[16:]
            res.append(acc)
        qbuf[here, :] = res[0]
        signal = res[1] * res[2]
        sbuf[here, :] = signal
        sbf[here, :] = signal.astype(BF)

    @pl.loop(1, SPAN // 32)
    def _(block):
        short(block)

    arrived(halo, hr.at[0])
    before = jnp.where(lax.broadcast_in_dim(c, (16, WIDTH), ()) > 0, halo[...].astype(F32), 0.0)
    for i in range(3):
        ext[i, pl.ds(0, 16), :] = pltpu.roll(before, 14 - 2 * i, 0).astype(BF)
    short(0)
    for part in range(2):
        cols = pl.ds(part * HALF, HALF)
        ssend[cols, :] = nt(eye[...], sbf[:, cols]).astype(BF)
    for b in range(2):
        for k, peer in enumerate(peers):
            start(rows32(ssend, 2 * peer[0] + b), rows32(srecv.at[b], c), ss.at[b, k], sr.at[b, c], peer)
        pltpu.make_async_copy(rows32(ssend, 2 * c + b), rows32(srecv.at[b], c), sr.at[b, c]).start()

    get_w = []
    for p in range(8):
        keep_cols = pl.ds(pl.multiple_of((2 * p + core) * WIDTH, WIDTH), WIDTH)
        give_cols = pl.ds(pl.multiple_of((2 * p + 1 - core) * WIDTH, WIDTH), WIDTH)
        copy = pltpu.make_async_copy(weight.at[:, keep_cols], wbuf.at[p, mine], wloc.at[p])
        copy.start()
        get_w.append(copy)
        start(weight.at[:, give_cols], wbuf.at[p, mine], ws.at[p], wr.at[p], partner)

    get_fwd.wait()

    def transform(block, spec):
        @pl.loop(0, 4)
        def _(n):
            cols = pl.ds(pl.multiple_of(n * HALF, HALF), HALF)
            spec[:, cols] = mm(block[...], fwd[0, :, cols]) + mm(block[...], fwd[1, :, cols])

    for k in range(NCTX):
        arrived(rows64(frecv, k), fr.at[k])
    transform(frecv, spec_h)

    def products(b):
        for lane in range(4):
            re, im = pl.ds(lane * 128, 128), pl.ds(SPAN + lane * 128, 128)

            @pl.loop(0, BATCH // 8)
            def _(r, re=re, im=im, odd=lane >= 2):
                def rows(block, size, base):
                    return pl.ds(pl.multiple_of(block * size + base + r * 8, 8), 8)

                h_re = [spec_h[rows(d, OWN, b * BATCH), re] for d in range(NCTX)]
                h_im = [spec_h[rows(d, OWN, b * BATCH), im] for d in range(NCTX)]
                if odd:
                    g_re = [h_re[0]] + [h_re[d] + h_im[d - 1] for d in range(1, NCTX)]
                    g_im = [h_im[0]] + [h_im[d] - h_re[d - 1] for d in range(1, NCTX)]
                else:
                    g_re = [h_re[0]] + [h_re[d] - h_im[d - 1] for d in range(1, NCTX)]
                    g_im = [h_im[0]] + [h_im[d] + h_re[d - 1] for d in range(1, NCTX)]
                x_re = [spec_x[b, rows(j, BATCH, 0), re] for j in range(NCTX)]
                x_im = [spec_x[b, rows(j, BATCH, 0), im] for j in range(NCTX)]
                for i in range(NCTX):
                    y_re = x_re[0] * g_re[i] - x_im[0] * g_im[i]
                    y_im = x_re[0] * g_im[i] + x_im[0] * g_re[i]
                    for j in range(1, i + 1):
                        y_re = y_re + x_re[j] * g_re[i - j] - x_im[j] * g_im[i - j]
                        y_im = y_im + x_re[j] * g_im[i - j] + x_im[j] * g_re[i - j]
                    spec_y[b, rows(i, BATCH, 0), re] = y_re
                    spec_y[b, rows(i, BATCH, 0), im] = y_im

        @pl.loop(0, 8)
        def _(r):
            rows = pl.ds(pl.multiple_of(r * 32, 32), 32)
            value = spec_y[b, rows, :]
            high = value.astype(BF)
            yhi[b, rows, :] = high
            ylo[b, rows, :] = (value - high.astype(F32)).astype(BF)

    def inverse(b, h):
        cols = pl.ds(h * HALF, HALF)
        back = mm(yhi[b], inv[0, :, cols]) + mm(ylo[b], inv[0, :, cols]) + mm(yhi[b], inv[1, :, cols])
        csend[h, b] = back.astype(BF)
        for k, peer in enumerate(peers):
            start(
                rows32(csend.at[h, b], peer[0]), rows32(crecv.at[h], 2 * c + b),
                cs.at[h, b, k], cr.at[h, b, c], peer,
            )
        pltpu.make_async_copy(
            rows32(csend.at[h, b], c), rows32(crecv.at[h], 2 * c + b), cr.at[h, b, c]
        ).start()

    get_inv.wait()
    for b in range(2):
        for k in range(NCTX):
            arrived(rows32(srecv.at[b], k), sr.at[b, k])
        transform(srecv.at[b], spec_x.at[b])
        products(b)
        inverse(b, 0)
    for b in range(2):
        inverse(b, 1)

    def gate(h):
        for b in range(2):
            for k in range(NCTX):
                arrived(rows32(crecv.at[h], 2 * k + b), cr.at[h, b, k])
        rows = pl.ds(h * HALF, HALF)
        conv = nt(eye[...], crecv[h])
        gated = qbuf[rows, :] * (conv + skip[...] * sbuf[rows, :])
        gbuf[h, core] = gated.astype(BF)
        start(gbuf.at[h, core], gbuf.at[h, core], gs.at[h], gr.at[h], partner)

    def met(h):
        arrived(gbuf.at[h, 1 - core], gr.at[h])

    def project(h, dz, other):
        p = ((z + dz) % 4) * 2 + (xh if other == 0 else 1 - xh)
        return mm(gbuf[h, 0], wbuf[p, :WIDTH, :]) + mm(gbuf[h, 1], wbuf[p, WIDTH:, :])

    top, low = pl.ds(0, QUART), pl.ds(QUART, QUART)

    gate(0)
    for p in range(8):
        get_w[p].wait()
        arrived(wbuf.at[p, pl.ds(pl.multiple_of((1 - core) * WIDTH, WIDTH), WIDTH)], wr.at[p])
    met(0)
    for dz in (2, 1, 3, 0):
        xsend[dz] = project(0, dz, 1).astype(BF)
        start(xsend.at[dz], xrecv.at[dz], xs.at[dz], xr.at[dz], across)
    gate(1)
    met(1)
    for o in (1, 0):
        z1send[o] = project(1, 2, o).astype(BF)
        start(z1send.at[o, top], z1recv.at[0, o], z1s.at[0, o], z1r.at[0, o], up)
        start(z1send.at[o, low], z1recv.at[1, o], z1s.at[1, o], z1r.at[1, o], down)

    def second(o):
        for d, dz, rows, device in ((0, 1, top, up), (1, 3, low, down)):
            keep[...] = project(1, dz, o)
            arrived(z1recv.at[d, o], z1r.at[d, o])
            keep[rows, :] += z1recv[d, o].astype(F32)
            z2send[d, o] = keep[...].astype(BF)
            start(z2send.at[d, o], z2recv.at[d, o], z2s.at[d, o], z2r.at[d, o], device)

    def summed(dz):
        keep[...] = project(0, dz, 0)
        arrived(xrecv.at[dz], xr.at[dz])
        keep[...] += xrecv[dz].astype(F32)

    def forward(d, dz, rows, device):
        summed(dz)
        arrived(s1recv.at[d], s1r.at[d])
        keep[rows, :] += s1recv[d].astype(F32)
        s2send[d] = keep[...].astype(BF)
        start(s2send.at[d], s2recv.at[d], s2s.at[d], s2r.at[d], device)

    def gathered(o):
        keep[...] = project(1, 0, o)
        for d in range(2):
            arrived(z2recv.at[d, o], z2r.at[d, o])
        keep[...] += z2recv[0, o].astype(F32) + z2recv[1, o].astype(F32)

    second(1)
    summed(2)
    s1send[...] = keep[...].astype(BF)
    start(s1send.at[top], s1recv.at[0], s1s.at[0], s1r.at[0], up)
    start(s1send.at[low], s1recv.at[1], s1s.at[1], s1r.at[1], down)
    second(0)
    forward(0, 1, top, up)
    gathered(1)
    zxsend[...] = keep[...].astype(BF)
    start(zxsend, zxrecv, zxs.at[0], zxr.at[0], across)
    forward(1, 3, low, down)
    summed(0)
    for d in range(2):
        arrived(s2recv.at[d], s2r.at[d])
    out[pl.ds(0, HALF), :] = (keep[...] + s2recv[0].astype(F32) + s2recv[1].astype(F32)).astype(BF)
    gathered(0)
    arrived(zxrecv, zxr.at[0])
    out[pl.ds(HALF, HALF), :] = (keep[...] + zxrecv[...].astype(F32)).astype(BF)
    for copy in sent:
        copy.wait_send()


def per_device(features, short_weight, long_filter, lengths, skip_gain, out_weight):
    forward, inverse = tables()
    dma = pltpu.SemaphoreType.DMA
    vm = pltpu.VMEM
    block = (HALF, WIDTH)
    scratch = [
        vm((3, 16 + SPAN, WIDTH), BF), vm((16, WIDTH), BF), vm((16, WIDTH), BF),
        vm((SPAN, WIDTH), BF), vm((WIDTH, SPAN), BF), vm((WIDTH, SPAN), BF),
        vm((SPAN, WIDTH), BF), vm((WIDTH, SPAN), BF), vm((2, WIDTH // 2, SPAN), BF),
        vm((SPAN, WIDTH), F32), vm((SPAN, WIDTH), F32),
        vm((2, SPAN, 2 * SPAN), BF), vm((2, 2 * SPAN, SPAN), BF), vm((HALF, HALF), BF),
        vm((WIDTH, 2 * SPAN), F32), vm((2, WIDTH // 2, 2 * SPAN), F32), vm((2, WIDTH // 2, 2 * SPAN), F32),
        vm((2, WIDTH // 2, 2 * SPAN), BF), vm((2, WIDTH // 2, 2 * SPAN), BF),
        vm((2, 2, WIDTH // 2, HALF), BF), vm((2, WIDTH, HALF), BF),
        vm((2, 2) + block, BF), vm((8, 2 * WIDTH, WIDTH), BF),
        vm((4,) + block, BF), vm((4,) + block, BF),
        vm((2,) + block, BF), vm((2, 2, QUART, WIDTH), BF),
        vm((2, 2) + block, BF), vm((2, 2) + block, BF),
        vm(block, BF), vm(block, BF),
        vm(block, BF), vm((2, QUART, WIDTH), BF),
        vm((2,) + block, BF), vm((2,) + block, BF), vm(block, F32),
        dma((4,)), dma((8,)), dma((1,)), dma((1,)),
        dma((7,)), dma((8,)), dma((2, 7)), dma((2, 8)), dma((8,)), dma((8,)),
        dma((2, 2, 7)), dma((2, 2, 8)), dma((2,)), dma((2,)),
        dma((4,)), dma((4,)), dma((2, 2)), dma((2, 2)), dma((2, 2)), dma((2, 2)),
        dma((1,)), dma((1,)), dma((2,)), dma((2,)), dma((2,)), dma((2,)),
    ]
    hbm = pl.BlockSpec(memory_space=pl.ANY)
    near = pl.BlockSpec(memory_space=pltpu.VMEM)
    return pl.pallas_call(
        kernel,
        out_shape=jax.ShapeDtypeStruct((SPAN, WIDTH), BF),
        in_specs=[pl.BlockSpec(memory_space=pltpu.SMEM), near, near, hbm, hbm, hbm, hbm, hbm],
        out_specs=near,
        scratch_shapes=scratch,
        name="hyena",
        compiler_params=pltpu.CompilerParams(
            collective_id=0, has_side_effects=True, vmem_limit_bytes=56 * 2**20
        ),
    )(
        lengths, short_weight, skip_gain.reshape(1, WIDTH), features, long_filter, out_weight,
        jnp.asarray(forward), jnp.asarray(inverse),
    )


def solution(mesh):
    return jax.shard_map(
        per_device,
        mesh=mesh,
        in_specs=(
            P(None, "ctx", "grp"),
            P(None, None, "grp"),
            P("ctx", "grp"),
            P(),
            P("grp"),
            P("grp", None),
        ),
        out_specs=P("ctx", "grp"),
        check_vma=False,
    )
```

```python
import numpy as np

import jax
import jax.numpy as jnp
import ml_dtypes
from jax import lax
from jax.experimental import pallas as pl
from jax.experimental.pallas import tpu as pltpu
from jax.sharding import PartitionSpec as P

GROUP_CH = 256
SPAN = 512
WIDTH = 512
NCTX = 8
OWN = WIDTH // NCTX
BATCHES = ((0, 32), (32, 32))
HALF = SPAN // 2
CHUNKS = ((0, 128), (128, 128), (256, 256))
EARLY = 384
BF = jnp.bfloat16
F32 = jnp.float32
MESH = pl.DeviceIdType.MESH


def tables():
    freq = np.concatenate([np.arange(0, SPAN, 2), np.arange(1, SPAN, 2)])
    angle = np.pi * ((np.arange(SPAN)[:, None] * (2 * freq + 1)[None, :]) % (4 * SPAN)) / (2 * SPAN)
    forward = np.concatenate([np.cos(angle), -np.sin(angle)], axis=1)
    high = forward.astype(ml_dtypes.bfloat16)
    low = (forward - high.astype(np.float64)).astype(ml_dtypes.bfloat16)
    scale = ml_dtypes.bfloat16(1.0 / SPAN)
    return (
        np.stack([high, low]),
        np.stack([np.ascontiguousarray(high.T) * scale, np.ascontiguousarray(low.T) * scale]),
    )


def nt(lhs, rhs):
    return lax.dot_general(lhs, rhs, (((1,), (1,)), ((), ())), preferred_element_type=F32)


def mm(lhs, rhs):
    return jnp.dot(lhs, rhs, preferred_element_type=F32)


def kernel(
    lens, sw, skip, feat, filt, weight, fwd_hbm, inv_hbm,
    out,
    ext, edge, halo, ftmp, fsend, frecv, sbf, ssend, srecv, qbuf, sbuf, fwd, inv, eye,
    spec_h, spec_x, spec_y, yhi, ylo, csend0, csend1, csend2, crecv0, crecv1, crecv2, gbuf, wbuf,
    za1, za1r, za2, za2r, zax, zaxr, zb1, zb1r, zb2, zb2r, zbx, zbxr,
    xa, xar, xa1, xa1r, xa2, xa2r, xb, xbr, xb1, xb1r, xb2, xb2r, keep_a, keep_b, keep_c, keep_d,
    loc, wloc, hs, hr, fs, fr, ss, sr, ws, wr, cs, cr, gs, gr,
    xs, xr, z1s, z1r, z2s, z2r, zxs, zxr, s1s, s1r, s2s, s2r,
):
    c, g = lax.axis_index("ctx"), lax.axis_index("grp")
    z, xh, core = g // 4, (g // 2) % 2, g % 2
    partner = (c, g + 1 - 2 * core)
    across = (c, g + 2 - 4 * xh)
    up = (c, ((z + 1) % 4) * 4 + xh * 2 + core)
    down = (c, ((z + 3) % 4) * 4 + xh * 2 + core)

    def remote(src, dst, send, recv, device):
        return pltpu.make_async_remote_copy(
            src_ref=src, dst_ref=dst, send_sem=send, recv_sem=recv, device_id=device, device_id_type=MESH
        )

    sent = []

    def start(*args):
        copy = remote(*args)
        copy.start()
        sent.append(copy)
        return copy

    def arrived(dst, recv):
        remote(dst, dst, hs.at[0], recv, partner).wait_recv()

    def rows64(ref, index):
        return ref.at[pl.ds(pl.multiple_of(index * OWN, OWN), OWN)]

    def rows16(ref, base, size):
        return ref.at[pl.ds(pl.multiple_of(base, 16), size)]

    get_filt = pltpu.make_async_copy(filt, ftmp, loc.at[0])
    get_feat = pltpu.make_async_copy(feat, ext.at[:, pl.ds(16, SPAN)], loc.at[1])
    get_fwd = pltpu.make_async_copy(fwd_hbm, fwd, loc.at[2])
    get_inv = pltpu.make_async_copy(inv_hbm, inv, loc.at[3])
    get_filt.start()
    get_feat.start()
    get_fwd.start()
    get_inv.start()
    mine = pl.ds(pl.multiple_of(core * WIDTH, WIDTH), WIDTH)

    barrier = pltpu.get_barrier_semaphore()
    peers = [(lax.rem(c + k, NCTX), g) for k in range(1, NCTX)]
    for device in peers + [partner, across, up, down]:
        pl.semaphore_signal(barrier, inc=1, device_id=device, device_id_type=MESH)

    eye[...] = (
        lax.broadcasted_iota(jnp.int32, (HALF, HALF), 0) == lax.broadcasted_iota(jnp.int32, (HALF, HALF), 1)
    ).astype(F32).astype(BF)
    get_filt.wait()
    for part in range(WIDTH // GROUP_CH):
        length = lens[2 * g + part]
        cols = pl.ds(part * GROUP_CH, GROUP_CH)
        lag = c * SPAN + lax.broadcasted_iota(jnp.int32, (SPAN, GROUP_CH), 0)
        cut = jnp.where(lag < length, ftmp[:, cols].astype(F32), 0.0).astype(BF)
        fsend[cols, :] = nt(eye[...], cut).astype(BF)

    get_feat.wait()
    row = lax.broadcasted_iota(jnp.int32, (16, WIDTH), 0)
    packed = jnp.zeros((16, WIDTH), F32)
    for i in range(3):
        last = pltpu.roll(ext[i, pl.ds(SPAN, 16), :].astype(F32), 2 + 2 * i, 0)
        packed = jnp.where(row // 2 == i, last, packed)
    edge[...] = packed.astype(BF)

    pl.semaphore_wait(barrier, len(peers) + 4)
    start(edge, halo, hs.at[0], hr.at[0], peers[0])
    for k, peer in enumerate(peers):
        start(rows64(fsend, peer[0]), rows64(frecv, c), fs.at[k], fr.at[c], peer)
    own_f = pltpu.make_async_copy(rows64(fsend, c), rows64(frecv, c), fr.at[c])
    own_f.start()


    def short(block):
        base = pl.multiple_of(block * 32, 32)
        here = pl.ds(base, 32)
        res = []
        for i in range(3):
            v = ext[i, pl.ds(base, 48), :].astype(F32)
            acc = sw[0, i : i + 1, :] * v[16:]
            acc = acc + sw[1, i : i + 1, :] * pltpu.roll(v, 1, 0)[16:]
            acc = acc + sw[2, i : i + 1, :] * pltpu.roll(v, 2, 0)[16:]
            res.append(acc)
        qbuf[here, :] = res[0]
        signal = res[1] * res[2]
        sbuf[here, :] = signal
        sbf[here, :] = signal.astype(BF)

    @pl.loop(1, SPAN // 32)
    def _(block):
        short(block)

    arrived(halo, hr.at[0])
    before = jnp.where(lax.broadcast_in_dim(c, (16, WIDTH), ()) > 0, halo[...].astype(F32), 0.0)
    for i in range(3):
        ext[i, pl.ds(0, 16), :] = pltpu.roll(before, 14 - 2 * i, 0).astype(BF)
    short(0)
    for part in range(2):
        cols = pl.ds(part * HALF, HALF)
        ssend[cols, :] = nt(eye[...], sbf[:, cols]).astype(BF)
    def send_signal(b):
        off, size = BATCHES[b]
        for k, peer in enumerate(peers):
            start(
                rows16(ssend, peer[0] * OWN + off, size), rows16(srecv, NCTX * off + c * size, size),
                ss.at[b, k], sr.at[b, c], peer,
            )
        pltpu.make_async_copy(
            rows16(ssend, c * OWN + off, size), rows16(srecv, NCTX * off + c * size, size), sr.at[b, c]
        ).start()

    send_signal(0)

    get_w = []
    for p in range(8):
        keep_cols = pl.ds(pl.multiple_of((2 * p + core) * WIDTH, WIDTH), WIDTH)
        give_cols = pl.ds(pl.multiple_of((2 * p + 1 - core) * WIDTH, WIDTH), WIDTH)
        copy = pltpu.make_async_copy(weight.at[:, keep_cols], wbuf.at[p, mine], wloc.at[p])
        copy.start()
        get_w.append(copy)
        start(weight.at[:, give_cols], wbuf.at[p, mine], ws.at[p], wr.at[p], partner)

    get_fwd.wait()

    def transform(block, spec):
        for n in range(0, 2 * SPAN, HALF):
            cols = pl.ds(n, HALF)
            spec[:, cols] = mm(block[...], fwd[0, :, cols]) + mm(block[...], fwd[1, :, cols])

    for k in range(NCTX):
        arrived(rows64(frecv, k), fr.at[k])
    send_signal(1)
    transform(frecv, spec_h)

    def products(off, size):
        for lane in range(4):
            re, im = pl.ds(lane * 128, 128), pl.ds(SPAN + lane * 128, 128)

            @pl.loop(0, size // 8)
            def _(r, re=re, im=im, odd=lane >= 2):
                def taps(d):
                    return pl.ds(pl.multiple_of(d * OWN + off + r * 8, 8), 8)

                def rows(j):
                    return pl.ds(pl.multiple_of(NCTX * off + j * size + r * 8, 8), 8)

                h_re = [spec_h[taps(d), re] for d in range(NCTX)]
                h_im = [spec_h[taps(d), im] for d in range(NCTX)]
                if odd:
                    g_re = [h_re[0]] + [h_re[d] + h_im[d - 1] for d in range(1, NCTX)]
                    g_im = [h_im[0]] + [h_im[d] - h_re[d - 1] for d in range(1, NCTX)]
                else:
                    g_re = [h_re[0]] + [h_re[d] - h_im[d - 1] for d in range(1, NCTX)]
                    g_im = [h_im[0]] + [h_im[d] + h_re[d - 1] for d in range(1, NCTX)]
                x_re = [spec_x[rows(j), re] for j in range(NCTX)]
                x_im = [spec_x[rows(j), im] for j in range(NCTX)]
                for i in range(NCTX):
                    y_re = x_re[0] * g_re[i] - x_im[0] * g_im[i]
                    y_im = x_re[0] * g_im[i] + x_im[0] * g_re[i]
                    for j in range(1, i + 1):
                        y_re = y_re + x_re[j] * g_re[i - j] - x_im[j] * g_im[i - j]
                        y_im = y_im + x_re[j] * g_im[i - j] + x_im[j] * g_re[i - j]
                    spec_y[rows(i), re] = y_re
                    spec_y[rows(i), im] = y_im

        @pl.loop(0, NCTX * size // 32)
        def _(r):
            rows = pl.ds(pl.multiple_of(NCTX * off + r * 32, 32), 32)
            value = spec_y[rows, :]
            high = value.astype(BF)
            yhi[rows, :] = high
            ylo[rows, :] = (value - high.astype(F32)).astype(BF)

    csend, crecv = (csend0, csend1, csend2), (crecv0, crecv1, crecv2)

    def inverse(t, off, size):
        rows, cols = pl.ds(NCTX * off, NCTX * size), pl.ds(*CHUNKS[t])
        back = mm(yhi[rows, :], inv[0, :, cols]) + mm(ylo[rows, :], inv[0, :, cols]) + mm(yhi[rows, :], inv[1, :, cols])
        for i in range(NCTX):
            csend[t][pl.ds(i * OWN + off, size), :] = back[i * size : (i + 1) * size].astype(BF)

    def give_back(t, b, off, size):
        for k, peer in enumerate(peers):
            start(
                rows16(csend[t], peer[0] * OWN + off, size), rows16(crecv[t], c * OWN + off, size),
                cs.at[t, b, k], cr.at[t, b, c], peer,
            )
        pltpu.make_async_copy(
            rows16(csend[t], c * OWN + off, size), rows16(crecv[t], c * OWN + off, size), cr.at[t, b, c]
        ).start()

    get_inv.wait()
    for b, (off, size) in enumerate(BATCHES):
        for k in range(NCTX):
            arrived(rows16(srecv, NCTX * off + k * size, size), sr.at[b, k])
        batch = pl.ds(NCTX * off, NCTX * size)
        transform(srecv.at[batch], spec_x.at[batch])
        products(off, size)
        inverse(0, off, size)
        give_back(0, b, off, size)
    for t in range(1, len(CHUNKS)):
        inverse(t, 0, BATCHES[0][1])
        for off, size in BATCHES[1:]:
            inverse(t, off, size)
        give_back(t, 0, 0, OWN)

    def gate(t):
        for b, (off, size) in enumerate(BATCHES if t == 0 else ((0, OWN),)):
            for k in range(NCTX):
                arrived(rows16(crecv[t], k * OWN + off, size), cr.at[t, b, k])
        rows = pl.ds(*CHUNKS[t])
        conv = nt(eye[: CHUNKS[t][1], : CHUNKS[t][1]], crecv[t][...])
        gated = qbuf[rows, :] * (conv + skip[...] * sbuf[rows, :])
        gbuf[core, rows] = gated.astype(BF)
        start(gbuf.at[core, rows], gbuf.at[core, rows], gs.at[t], gr.at[t], partner)

    def met(t):
        arrived(gbuf.at[1 - core, pl.ds(*CHUNKS[t])], gr.at[t])

    def place(dz, other):
        return ((z + dz) % 4) * 2 + (1 - xh if other else xh)

    def project(t, dz, other, cols):
        p, rows = place(dz, other), pl.ds(*CHUNKS[t])
        return mm(gbuf[0, rows], wbuf[p, :WIDTH, cols]) + mm(gbuf[1, rows], wbuf[p, WIDTH:, cols])

    every, early, late = slice(0, WIDTH), slice(0, EARLY), slice(EARLY, WIDTH)
    z_parts = (
        (0, every, za1, za1r, za2, za2r, zax, zaxr, keep_a),
        (2, early, zb1, zb1r, zb2, zb2r, zbx, zbxr, keep_b),
    )
    x_parts = (
        (1, every, xa, xar, xa1, xa1r, xa2, xa2r, keep_c),
        (2, late, xb, xbr, xb1, xb1r, xb2, xb2r, keep_d),
    )

    def halves(t):
        size = CHUNKS[t][1] // 2
        return pl.ds(0, size), pl.ds(size, size)

    def first(q, o, value):
        t, _, send, recv, *_ = z_parts[q]
        top, low = halves(t)
        send[o] = value.astype(BF)
        start(send.at[o, top], recv.at[0, o], z1s.at[q, 0, o], z1r.at[q, 0, o], up)
        start(send.at[o, low], recv.at[1, o], z1s.at[q, 1, o], z1r.at[q, 1, o], down)

    def second(q, o):
        t, cols, _, had, send, recv, _, _, keep = z_parts[q]
        top, low = halves(t)
        for d, dz, rows, device in ((0, 1, top, up), (1, 3, low, down)):
            keep[...] = project(t, dz, o, cols)
            arrived(had.at[d, o], z1r.at[q, d, o])
            keep[rows, :] += had[d, o].astype(F32)
            send[d, o] = keep[...].astype(BF)
            start(send.at[d, o], recv.at[d, o], z2s.at[q, d, o], z2r.at[q, d, o], device)

    def third(q):
        t, cols, _, _, _, had, send, recv, keep = z_parts[q]
        keep[...] = project(t, 0, 1, cols)
        for d in range(2):
            arrived(had.at[d, 1], z2r.at[q, d, 1])
        send[...] = (keep[...] + had[0, 1].astype(F32) + had[1, 1].astype(F32)).astype(BF)
        start(send, recv, zxs.at[q], zxr.at[q], across)

    def last(q):
        t, cols, _, _, _, had, _, recv, keep = z_parts[q]
        for d in range(2):
            arrived(had.at[d, 0], z2r.at[q, d, 0])
        arrived(recv, zxr.at[q])
        total = keep[...] + had[0, 0].astype(F32) + had[1, 0].astype(F32) + recv[...].astype(F32)
        out[pl.ds(*CHUNKS[t]), cols] = total.astype(BF)

    def over_x(q, dz):
        t, cols, send, recv, *_ = x_parts[q]
        send[dz] = project(t, dz, 1, cols).astype(BF)
        start(send.at[dz], recv.at[dz], xs.at[q, dz], xr.at[q, dz], across)

    def summed(q, dz):
        t, cols, _, had, *_, keep = x_parts[q]
        keep[...] = project(t, dz, 0, cols)
        arrived(had.at[dz], xr.at[q, dz])
        keep[...] += had[dz].astype(F32)

    def apart(q):
        t, _, _, _, send, recv, _, _, keep = x_parts[q]
        top, low = halves(t)
        summed(q, 2)
        send[...] = keep[...].astype(BF)
        start(send.at[top], recv.at[0], s1s.at[q, 0], s1r.at[q, 0], up)
        start(send.at[low], recv.at[1], s1s.at[q, 1], s1r.at[q, 1], down)

    def forward(q):
        t, _, _, _, _, had, send, recv, keep = x_parts[q]
        top, low = halves(t)
        for d, dz, rows, device in ((0, 1, top, up), (1, 3, low, down)):
            summed(q, dz)
            arrived(had.at[d], s1r.at[q, d])
            keep[rows, :] += had[d].astype(F32)
            send[d] = keep[...].astype(BF)
            start(send.at[d], recv.at[d], s2s.at[q, d], s2r.at[q, d], device)

    def close(q):
        t, cols, _, _, _, _, _, had, keep = x_parts[q]
        for d in range(2):
            arrived(had.at[d], s2r.at[q, d])
        out[pl.ds(*CHUNKS[t]), cols] = (keep[...] + had[0].astype(F32) + had[1].astype(F32)).astype(BF)

    gate(0)
    for p in range(8):
        get_w[p].wait()
        arrived(wbuf.at[p, pl.ds(pl.multiple_of((1 - core) * WIDTH, WIDTH), WIDTH)], wr.at[p])
    other, rows = pl.ds(pl.multiple_of((1 - core) * WIDTH, WIDTH), WIDTH), pl.ds(*CHUNKS[0])
    for o, keep in ((1, keep_a), (0, keep_c)):
        keep[...] = mm(gbuf[core, rows], wbuf[place(2, o), mine, :])
    met(0)
    for o, keep in ((1, keep_a), (0, keep_c)):
        first(0, o, keep[...] + mm(gbuf[1 - core, rows], wbuf[place(2, o), other, :]))
    gate(1)
    met(1)
    for dz in (2, 1, 3):
        over_x(0, dz)
    second(0, 1)
    gate(2)
    met(2)
    for o in (1, 0):
        first(1, o, project(2, 2, o, early))
    for dz in (2, 1, 3):
        over_x(1, dz)
    over_x(0, 0)
    over_x(1, 0)
    apart(0)
    third(0)
    second(1, 1)
    apart(1)
    second(0, 0)
    forward(0)
    second(1, 0)
    third(1)
    forward(1)
    for t, cols, *_, keep in z_parts:
        keep[...] = project(t, 0, 0, cols)
    for q in range(2):
        summed(q, 0)
    last(0)
    close(0)
    last(1)
    close(1)
    for copy in sent:
        copy.wait_send()


def per_device(features, short_weight, long_filter, lengths, skip_gain, out_weight):
    forward, inverse = tables()
    dma = pltpu.SemaphoreType.DMA
    vm = pltpu.VMEM
    sizes = [size for _, size in CHUNKS]
    z_shapes = ((sizes[0], WIDTH), (sizes[2], EARLY))
    x_shapes = ((sizes[1], WIDTH), (sizes[2], WIDTH - EARLY))
    scratch = [
        vm((3, 16 + SPAN, WIDTH), BF), vm((16, WIDTH), BF), vm((16, WIDTH), BF),
        vm((SPAN, WIDTH), BF), vm((WIDTH, SPAN), BF), vm((WIDTH, SPAN), BF),
        vm((SPAN, WIDTH), BF), vm((WIDTH, SPAN), BF), vm((WIDTH, SPAN), BF),
        vm((SPAN, WIDTH), F32), vm((SPAN, WIDTH), F32),
        vm((2, SPAN, 2 * SPAN), BF), vm((2, 2 * SPAN, SPAN), BF), vm((HALF, HALF), BF),
        vm((WIDTH, 2 * SPAN), F32), vm((WIDTH, 2 * SPAN), F32), vm((WIDTH, 2 * SPAN), F32),
        vm((WIDTH, 2 * SPAN), BF), vm((WIDTH, 2 * SPAN), BF),
        *[vm((WIDTH, size), BF) for size in sizes], *[vm((WIDTH, size), BF) for size in sizes],
        vm((2, SPAN, WIDTH), BF), vm((8, 2 * WIDTH, WIDTH), BF),
    ]
    for rows, cols in z_shapes:
        scratch += [
            vm((2, rows, cols), BF), vm((2, 2, rows // 2, cols), BF),
            vm((2, 2, rows, cols), BF), vm((2, 2, rows, cols), BF),
            vm((rows, cols), BF), vm((rows, cols), BF),
        ]
    for rows, cols in x_shapes:
        scratch += [
            vm((4, rows, cols), BF), vm((4, rows, cols), BF),
            vm((rows, cols), BF), vm((2, rows // 2, cols), BF),
            vm((2, rows, cols), BF), vm((2, rows, cols), BF),
        ]
    scratch += [
        *[vm(shape, F32) for shape in z_shapes + x_shapes],
        dma((4,)), dma((8,)), dma((1,)), dma((1,)),
        dma((7,)), dma((8,)), dma((2, 7)), dma((2, 8)), dma((8,)), dma((8,)),
        dma((3, 2, 7)), dma((3, 2, 8)), dma((3,)), dma((3,)),
        dma((2, 4)), dma((2, 4)), dma((2, 2, 2)), dma((2, 2, 2)), dma((2, 2, 2)), dma((2, 2, 2)),
        dma((2,)), dma((2,)), dma((2, 2)), dma((2, 2)), dma((2, 2)), dma((2, 2)),
    ]
    hbm = pl.BlockSpec(memory_space=pl.ANY)
    near = pl.BlockSpec(memory_space=pltpu.VMEM)
    return pl.pallas_call(
        kernel,
        out_shape=jax.ShapeDtypeStruct((SPAN, WIDTH), BF),
        in_specs=[pl.BlockSpec(memory_space=pltpu.SMEM), near, near, hbm, hbm, hbm, hbm, hbm],
        out_specs=near,
        scratch_shapes=scratch,
        name="hyena",
        compiler_params=pltpu.CompilerParams(
            collective_id=0, has_side_effects=True, vmem_limit_bytes=56 * 2**20
        ),
    )(
        lengths, short_weight, skip_gain.reshape(1, WIDTH), features, long_filter, out_weight,
        jnp.asarray(forward), jnp.asarray(inverse),
    )


def solution(mesh):
    return jax.shard_map(
        per_device,
        mesh=mesh,
        in_specs=(
            P(None, "ctx", "grp"),
            P(None, None, "grp"),
            P("ctx", "grp"),
            P(),
            P("grp"),
            P("grp", None),
        ),
        out_specs=P("ctx", "grp"),
        check_vma=False,
    )
```

```python
import numpy as np

import jax
import jax.numpy as jnp
import ml_dtypes
from jax import lax
from jax.experimental import pallas as pl
from jax.experimental.pallas import tpu as pltpu
from jax.sharding import PartitionSpec as P

GROUP_CH = 256
SPAN = 512
WIDTH = 512
NCTX = 8
OWN = WIDTH // NCTX
BATCHES = ((0, 32), (32, 32))
HALF = SPAN // 2
CHUNKS = ((0, 128), (128, 128), (256, 256))
EARLY = 384
BF = jnp.bfloat16
F32 = jnp.float32
MESH = pl.DeviceIdType.MESH


def tables():
    freq = np.concatenate([np.arange(0, SPAN, 2), np.arange(1, SPAN, 2)])
    angle = np.pi * ((np.arange(SPAN)[:, None] * (2 * freq + 1)[None, :]) % (4 * SPAN)) / (2 * SPAN)
    forward = np.concatenate([np.cos(angle), -np.sin(angle)], axis=1)
    high = forward.astype(ml_dtypes.bfloat16)
    low = (forward - high.astype(np.float64)).astype(ml_dtypes.bfloat16)
    scale = ml_dtypes.bfloat16(1.0 / SPAN)
    return (
        np.stack([high, low]),
        np.stack([np.ascontiguousarray(high.T) * scale, np.ascontiguousarray(low.T) * scale]),
    )


def nt(lhs, rhs):
    return lax.dot_general(lhs, rhs, (((1,), (1,)), ((), ())), preferred_element_type=F32)


def mm(lhs, rhs):
    return jnp.dot(lhs, rhs, preferred_element_type=F32)


def kernel(
    lens_hbm, sw_hbm, skip_hbm, feat, filt, weight, fwd_hbm, inv_hbm,
    out,
    lens, sw, skip, ext, edge, halo, ftmp, fsend, frecv, sbf, ssend, srecv, qbuf, sbuf, fwd, inv, eye,
    spec_h, spec_x, spec_y, yhi, ylo, csend0, csend1, csend2, crecv0, crecv1, crecv2, gbuf, wbuf,
    za1, za1r, za2, za2r, zax, zaxr, zb1, zb1r, zb2, zb2r, zbx, zbxr,
    xa, xar, xa1, xa1r, xa2, xa2r, xb, xbr, xb1, xb1r, xb2, xb2r, keep_a, keep_b, keep_c, keep_d,
    loc, wloc, hs, hr, fs, fr, ss, sr, ws, wr, cs, cr, gs, gr,
    xs, xr, z1s, z1r, z2s, z2r, zxs, zxr, s1s, s1r, s2s, s2r,
):
    c, g = lax.axis_index("ctx"), lax.axis_index("grp")
    z, xh, core = g // 4, (g // 2) % 2, g % 2
    partner = (c, g + 1 - 2 * core)
    across = (c, g + 2 - 4 * xh)
    up = (c, ((z + 1) % 4) * 4 + xh * 2 + core)
    down = (c, ((z + 3) % 4) * 4 + xh * 2 + core)

    def remote(src, dst, send, recv, device):
        return pltpu.make_async_remote_copy(
            src_ref=src, dst_ref=dst, send_sem=send, recv_sem=recv, device_id=device, device_id_type=MESH
        )

    sent = []

    def start(*args):
        copy = remote(*args)
        copy.start()
        sent.append(copy)
        return copy

    def arrived(dst, recv):
        remote(dst, dst, hs.at[0], recv, partner).wait_recv()

    def rows64(ref, index):
        return ref.at[pl.ds(pl.multiple_of(index * OWN, OWN), OWN)]

    def rows16(ref, base, size):
        return ref.at[pl.ds(pl.multiple_of(base, 16), size)]

    barrier = pltpu.get_barrier_semaphore()
    peers = [(lax.rem(c + k, NCTX), g) for k in range(1, NCTX)]
    for device in peers + [partner, across, up, down]:
        pl.semaphore_signal(barrier, inc=1, device_id=device, device_id_type=MESH)

    get_filt = pltpu.make_async_copy(filt, ftmp, loc.at[0])
    get_feat = pltpu.make_async_copy(feat, ext.at[:, pl.ds(16, SPAN)], loc.at[1])
    get_fwd = pltpu.make_async_copy(fwd_hbm, fwd, loc.at[2])
    get_inv = pltpu.make_async_copy(inv_hbm, inv, loc.at[3])
    get_lens = pltpu.make_async_copy(lens_hbm, lens, loc.at[4])
    get_sw = pltpu.make_async_copy(sw_hbm, sw, loc.at[5])
    get_skip = pltpu.make_async_copy(skip_hbm, skip, loc.at[6])
    get_lens.start()
    get_filt.start()
    get_feat.start()
    get_sw.start()
    get_skip.start()
    get_fwd.start()
    get_inv.start()
    mine = pl.ds(pl.multiple_of(core * WIDTH, WIDTH), WIDTH)

    eye[...] = (
        lax.broadcasted_iota(jnp.int32, (HALF, HALF), 0) == lax.broadcasted_iota(jnp.int32, (HALF, HALF), 1)
    ).astype(F32).astype(BF)
    get_lens.wait()
    get_filt.wait()
    for part in range(WIDTH // GROUP_CH):
        length = lens[2 * g + part]
        cols = pl.ds(part * GROUP_CH, GROUP_CH)
        lag = c * SPAN + lax.broadcasted_iota(jnp.int32, (SPAN, GROUP_CH), 0)
        cut = jnp.where(lag < length, ftmp[:, cols].astype(F32), 0.0).astype(BF)
        fsend[cols, :] = nt(eye[...], cut).astype(BF)

    get_feat.wait()
    row = lax.broadcasted_iota(jnp.int32, (16, WIDTH), 0)
    packed = jnp.zeros((16, WIDTH), F32)
    for i in range(3):
        last = pltpu.roll(ext[i, pl.ds(SPAN, 16), :].astype(F32), 2 + 2 * i, 0)
        packed = jnp.where(row // 2 == i, last, packed)
    edge[...] = packed.astype(BF)

    pl.semaphore_wait(barrier, len(peers) + 4)
    start(edge, halo, hs.at[0], hr.at[0], peers[0])
    for k, peer in enumerate(peers):
        start(rows64(fsend, peer[0]), rows64(frecv, c), fs.at[k], fr.at[c], peer)
    own_f = pltpu.make_async_copy(rows64(fsend, c), rows64(frecv, c), fr.at[c])
    own_f.start()


    def short(block):
        base = pl.multiple_of(block * 32, 32)
        here = pl.ds(base, 32)
        res = []
        for i in range(3):
            v = ext[i, pl.ds(base, 48), :].astype(F32)
            acc = sw[0, i : i + 1, :] * v[16:]
            acc = acc + sw[1, i : i + 1, :] * pltpu.roll(v, 1, 0)[16:]
            acc = acc + sw[2, i : i + 1, :] * pltpu.roll(v, 2, 0)[16:]
            res.append(acc)
        qbuf[here, :] = res[0]
        signal = res[1] * res[2]
        sbuf[here, :] = signal
        sbf[here, :] = signal.astype(BF)

    get_sw.wait()
    get_skip.wait()

    @pl.loop(1, SPAN // 32)
    def _(block):
        short(block)

    arrived(halo, hr.at[0])
    before = jnp.where(lax.broadcast_in_dim(c, (16, WIDTH), ()) > 0, halo[...].astype(F32), 0.0)
    for i in range(3):
        ext[i, pl.ds(0, 16), :] = pltpu.roll(before, 14 - 2 * i, 0).astype(BF)
    short(0)
    for part in range(2):
        cols = pl.ds(part * HALF, HALF)
        ssend[cols, :] = nt(eye[...], sbf[:, cols]).astype(BF)
    def send_signal(b):
        off, size = BATCHES[b]
        for k, peer in enumerate(peers):
            start(
                rows16(ssend, peer[0] * OWN + off, size), rows16(srecv, NCTX * off + c * size, size),
                ss.at[b, k], sr.at[b, c], peer,
            )
        pltpu.make_async_copy(
            rows16(ssend, c * OWN + off, size), rows16(srecv, NCTX * off + c * size, size), sr.at[b, c]
        ).start()

    send_signal(0)
    send_signal(1)

    get_w = []
    for p in range(8):
        keep_cols = pl.ds(pl.multiple_of((2 * p + core) * WIDTH, WIDTH), WIDTH)
        give_cols = pl.ds(pl.multiple_of((2 * p + 1 - core) * WIDTH, WIDTH), WIDTH)
        copy = pltpu.make_async_copy(weight.at[:, keep_cols], wbuf.at[p, mine], wloc.at[p])
        copy.start()
        get_w.append(copy)
        start(weight.at[:, give_cols], wbuf.at[p, mine], ws.at[p], wr.at[p], partner)

    get_fwd.wait()

    def transform(block, spec):
        for n in range(0, 2 * SPAN, HALF):
            cols = pl.ds(n, HALF)
            spec[:, cols] = mm(block[...], fwd[0, :, cols]) + mm(block[...], fwd[1, :, cols])

    for k in range(NCTX):
        arrived(rows64(frecv, k), fr.at[k])
    transform(frecv, spec_h)

    def products(off, size):
        for lane in range(4):
            re, im = pl.ds(lane * 128, 128), pl.ds(SPAN + lane * 128, 128)

            @pl.loop(0, size // 8)
            def _(r, re=re, im=im, odd=lane >= 2):
                def taps(d):
                    return pl.ds(pl.multiple_of(d * OWN + off + r * 8, 8), 8)

                def rows(j):
                    return pl.ds(pl.multiple_of(NCTX * off + j * size + r * 8, 8), 8)

                h_re = [spec_h[taps(d), re] for d in range(NCTX)]
                h_im = [spec_h[taps(d), im] for d in range(NCTX)]
                if odd:
                    g_re = [h_re[0]] + [h_re[d] + h_im[d - 1] for d in range(1, NCTX)]
                    g_im = [h_im[0]] + [h_im[d] - h_re[d - 1] for d in range(1, NCTX)]
                else:
                    g_re = [h_re[0]] + [h_re[d] - h_im[d - 1] for d in range(1, NCTX)]
                    g_im = [h_im[0]] + [h_im[d] + h_re[d - 1] for d in range(1, NCTX)]
                x_re = [spec_x[rows(j), re] for j in range(NCTX)]
                x_im = [spec_x[rows(j), im] for j in range(NCTX)]
                for i in range(NCTX):
                    y_re = x_re[0] * g_re[i] - x_im[0] * g_im[i]
                    y_im = x_re[0] * g_im[i] + x_im[0] * g_re[i]
                    for j in range(1, i + 1):
                        y_re = y_re + x_re[j] * g_re[i - j] - x_im[j] * g_im[i - j]
                        y_im = y_im + x_re[j] * g_im[i - j] + x_im[j] * g_re[i - j]
                    spec_y[rows(i), re] = y_re
                    spec_y[rows(i), im] = y_im

        @pl.loop(0, NCTX * size // 32)
        def _(r):
            rows = pl.ds(pl.multiple_of(NCTX * off + r * 32, 32), 32)
            value = spec_y[rows, :]
            high = value.astype(BF)
            yhi[rows, :] = high
            ylo[rows, :] = (value - high.astype(F32)).astype(BF)

    csend, crecv = (csend0, csend1, csend2), (crecv0, crecv1, crecv2)

    def inverse(t, off, size):
        rows, cols = pl.ds(NCTX * off, NCTX * size), pl.ds(*CHUNKS[t])
        back = mm(yhi[rows, :], inv[0, :, cols]) + mm(ylo[rows, :], inv[0, :, cols]) + mm(yhi[rows, :], inv[1, :, cols])
        for i in range(NCTX):
            csend[t][pl.ds(i * OWN + off, size), :] = back[i * size : (i + 1) * size].astype(BF)

    def give_back(t, b, off, size):
        for k, peer in enumerate(peers):
            start(
                rows16(csend[t], peer[0] * OWN + off, size), rows16(crecv[t], c * OWN + off, size),
                cs.at[t, b, k], cr.at[t, b, c], peer,
            )
        pltpu.make_async_copy(
            rows16(csend[t], c * OWN + off, size), rows16(crecv[t], c * OWN + off, size), cr.at[t, b, c]
        ).start()

    get_inv.wait()
    for b, (off, size) in enumerate(BATCHES):
        for k in range(NCTX):
            arrived(rows16(srecv, NCTX * off + k * size, size), sr.at[b, k])
        batch = pl.ds(NCTX * off, NCTX * size)
        transform(srecv.at[batch], spec_x.at[batch])
        products(off, size)
        inverse(0, off, size)
        give_back(0, b, off, size)
    for t in range(1, len(CHUNKS)):
        inverse(t, 0, BATCHES[0][1])
        for off, size in BATCHES[1:]:
            inverse(t, off, size)
        give_back(t, 0, 0, OWN)

    def gate(t):
        for b, (off, size) in enumerate(BATCHES if t == 0 else ((0, OWN),)):
            for k in range(NCTX):
                arrived(rows16(crecv[t], k * OWN + off, size), cr.at[t, b, k])
        rows = pl.ds(*CHUNKS[t])
        conv = nt(eye[: CHUNKS[t][1], : CHUNKS[t][1]], crecv[t][...])
        gated = qbuf[rows, :] * (conv + skip[...] * sbuf[rows, :])
        gbuf[core, rows] = gated.astype(BF)
        start(gbuf.at[core, rows], gbuf.at[core, rows], gs.at[t], gr.at[t], partner)

    def met(t):
        arrived(gbuf.at[1 - core, pl.ds(*CHUNKS[t])], gr.at[t])

    def place(dz, other):
        return ((z + dz) % 4) * 2 + (1 - xh if other else xh)

    def project(t, dz, other, cols):
        p, rows = place(dz, other), pl.ds(*CHUNKS[t])
        return mm(gbuf[0, rows], wbuf[p, :WIDTH, cols]) + mm(gbuf[1, rows], wbuf[p, WIDTH:, cols])

    every, early, late = slice(0, WIDTH), slice(0, EARLY), slice(EARLY, WIDTH)
    z_parts = (
        (0, every, za1, za1r, za2, za2r, zax, zaxr, keep_a),
        (2, early, zb1, zb1r, zb2, zb2r, zbx, zbxr, keep_b),
    )
    x_parts = (
        (1, every, xa, xar, xa1, xa1r, xa2, xa2r, keep_c),
        (2, late, xb, xbr, xb1, xb1r, xb2, xb2r, keep_d),
    )

    def halves(t):
        size = CHUNKS[t][1] // 2
        return pl.ds(0, size), pl.ds(size, size)

    def first(q, o, value):
        t, _, send, recv, *_ = z_parts[q]
        top, low = halves(t)
        send[o] = value.astype(BF)
        start(send.at[o, top], recv.at[0, o], z1s.at[q, 0, o], z1r.at[q, 0, o], up)
        start(send.at[o, low], recv.at[1, o], z1s.at[q, 1, o], z1r.at[q, 1, o], down)

    def second(q, o):
        t, cols, _, had, send, recv, _, _, keep = z_parts[q]
        top, low = halves(t)
        for d, dz, rows, device in ((0, 1, top, up), (1, 3, low, down)):
            keep[...] = project(t, dz, o, cols)
            arrived(had.at[d, o], z1r.at[q, d, o])
            keep[rows, :] += had[d, o].astype(F32)
            send[d, o] = keep[...].astype(BF)
            start(send.at[d, o], recv.at[d, o], z2s.at[q, d, o], z2r.at[q, d, o], device)

    def third(q):
        t, cols, _, _, _, had, send, recv, keep = z_parts[q]
        keep[...] = project(t, 0, 1, cols)
        for d in range(2):
            arrived(had.at[d, 1], z2r.at[q, d, 1])
        send[...] = (keep[...] + had[0, 1].astype(F32) + had[1, 1].astype(F32)).astype(BF)
        start(send, recv, zxs.at[q], zxr.at[q], across)

    def last(q):
        t, cols, _, _, _, had, _, recv, keep = z_parts[q]
        for d in range(2):
            arrived(had.at[d, 0], z2r.at[q, d, 0])
        arrived(recv, zxr.at[q])
        total = keep[...] + had[0, 0].astype(F32) + had[1, 0].astype(F32) + recv[...].astype(F32)
        out[pl.ds(*CHUNKS[t]), cols] = total.astype(BF)

    def over_x(q, dz):
        t, cols, send, recv, *_ = x_parts[q]
        send[dz] = project(t, dz, 1, cols).astype(BF)
        start(send.at[dz], recv.at[dz], xs.at[q, dz], xr.at[q, dz], across)

    def summed(q, dz):
        t, cols, _, had, *_, keep = x_parts[q]
        keep[...] = project(t, dz, 0, cols)
        arrived(had.at[dz], xr.at[q, dz])
        keep[...] += had[dz].astype(F32)

    def apart(q):
        t, _, _, _, send, recv, _, _, keep = x_parts[q]
        top, low = halves(t)
        summed(q, 2)
        send[...] = keep[...].astype(BF)
        start(send.at[top], recv.at[0], s1s.at[q, 0], s1r.at[q, 0], up)
        start(send.at[low], recv.at[1], s1s.at[q, 1], s1r.at[q, 1], down)

    def forward(q):
        t, _, _, _, _, had, send, recv, keep = x_parts[q]
        top, low = halves(t)
        for d, dz, rows, device in ((0, 1, top, up), (1, 3, low, down)):
            summed(q, dz)
            arrived(had.at[d], s1r.at[q, d])
            keep[rows, :] += had[d].astype(F32)
            send[d] = keep[...].astype(BF)
            start(send.at[d], recv.at[d], s2s.at[q, d], s2r.at[q, d], device)

    def close(q):
        t, cols, _, _, _, _, _, had, keep = x_parts[q]
        for d in range(2):
            arrived(had.at[d], s2r.at[q, d])
        out[pl.ds(*CHUNKS[t]), cols] = (keep[...] + had[0].astype(F32) + had[1].astype(F32)).astype(BF)

    gate(0)
    for p in range(8):
        get_w[p].wait()
        arrived(wbuf.at[p, pl.ds(pl.multiple_of((1 - core) * WIDTH, WIDTH), WIDTH)], wr.at[p])
    other, rows = pl.ds(pl.multiple_of((1 - core) * WIDTH, WIDTH), WIDTH), pl.ds(*CHUNKS[0])
    for o, keep in ((1, keep_a), (0, keep_c)):
        keep[...] = mm(gbuf[core, rows], wbuf[place(2, o), mine, :])
    met(0)
    for o, keep in ((1, keep_a), (0, keep_c)):
        first(0, o, keep[...] + mm(gbuf[1 - core, rows], wbuf[place(2, o), other, :]))
    gate(1)
    met(1)
    for dz in (2, 1, 3):
        over_x(0, dz)
    second(0, 1)
    gate(2)
    met(2)
    for o in (1, 0):
        first(1, o, project(2, 2, o, early))
    for dz in (2, 1, 3):
        over_x(1, dz)
    over_x(0, 0)
    over_x(1, 0)
    apart(0)
    third(0)
    second(1, 1)
    apart(1)
    second(0, 0)
    forward(0)
    second(1, 0)
    third(1)
    forward(1)
    for t, cols, *_, keep in z_parts:
        keep[...] = project(t, 0, 0, cols)
    for q in range(2):
        summed(q, 0)
    last(0)
    close(0)
    last(1)
    close(1)
    for copy in sent:
        copy.wait_send()


def per_device(features, short_weight, long_filter, lengths, skip_gain, out_weight):
    forward, inverse = tables()
    dma = pltpu.SemaphoreType.DMA
    vm = pltpu.VMEM
    sizes = [size for _, size in CHUNKS]
    z_shapes = ((sizes[0], WIDTH), (sizes[2], EARLY))
    x_shapes = ((sizes[1], WIDTH), (sizes[2], WIDTH - EARLY))
    scratch = [
        pltpu.SMEM((32,), jnp.int32), vm((3, 3, WIDTH), F32), vm((1, WIDTH), F32),
        vm((3, 16 + SPAN, WIDTH), BF), vm((16, WIDTH), BF), vm((16, WIDTH), BF),
        vm((SPAN, WIDTH), BF), vm((WIDTH, SPAN), BF), vm((WIDTH, SPAN), BF),
        vm((SPAN, WIDTH), BF), vm((WIDTH, SPAN), BF), vm((WIDTH, SPAN), BF),
        vm((SPAN, WIDTH), F32), vm((SPAN, WIDTH), F32),
        vm((2, SPAN, 2 * SPAN), BF), vm((2, 2 * SPAN, SPAN), BF), vm((HALF, HALF), BF),
        vm((WIDTH, 2 * SPAN), F32), vm((WIDTH, 2 * SPAN), F32), vm((WIDTH, 2 * SPAN), F32),
        vm((WIDTH, 2 * SPAN), BF), vm((WIDTH, 2 * SPAN), BF),
        *[vm((WIDTH, size), BF) for size in sizes], *[vm((WIDTH, size), BF) for size in sizes],
        vm((2, SPAN, WIDTH), BF), vm((8, 2 * WIDTH, WIDTH), BF),
    ]
    for rows, cols in z_shapes:
        scratch += [
            vm((2, rows, cols), BF), vm((2, 2, rows // 2, cols), BF),
            vm((2, 2, rows, cols), BF), vm((2, 2, rows, cols), BF),
            vm((rows, cols), BF), vm((rows, cols), BF),
        ]
    for rows, cols in x_shapes:
        scratch += [
            vm((4, rows, cols), BF), vm((4, rows, cols), BF),
            vm((rows, cols), BF), vm((2, rows // 2, cols), BF),
            vm((2, rows, cols), BF), vm((2, rows, cols), BF),
        ]
    scratch += [
        *[vm(shape, F32) for shape in z_shapes + x_shapes],
        dma((7,)), dma((8,)), dma((1,)), dma((1,)),
        dma((7,)), dma((8,)), dma((2, 7)), dma((2, 8)), dma((8,)), dma((8,)),
        dma((3, 2, 7)), dma((3, 2, 8)), dma((3,)), dma((3,)),
        dma((2, 4)), dma((2, 4)), dma((2, 2, 2)), dma((2, 2, 2)), dma((2, 2, 2)), dma((2, 2, 2)),
        dma((2,)), dma((2,)), dma((2, 2)), dma((2, 2)), dma((2, 2)), dma((2, 2)),
    ]
    hbm = pl.BlockSpec(memory_space=pl.ANY)
    near = pl.BlockSpec(memory_space=pltpu.VMEM)
    return pl.pallas_call(
        kernel,
        out_shape=pltpu.VMEM((SPAN, WIDTH), BF),
        in_specs=[hbm] * 8,
        out_specs=near,
        scratch_shapes=scratch,
        name="hyena",
        compiler_params=pltpu.CompilerParams(
            collective_id=0, has_side_effects=True, vmem_limit_bytes=56 * 2**20
        ),
    )(
        lengths, short_weight, skip_gain.reshape(1, WIDTH), features, long_filter, out_weight,
        jnp.asarray(forward), jnp.asarray(inverse),
    )


def solution(mesh):
    return jax.shard_map(
        per_device,
        mesh=mesh,
        in_specs=(
            P(None, "ctx", "grp"),
            P(None, None, "grp"),
            P("ctx", "grp"),
            P(),
            P("grp"),
            P("grp", None),
        ),
        out_specs=P("ctx", "grp"),
        check_vma=False,
    )
```

```python
import numpy as np

import jax
import jax.numpy as jnp
import ml_dtypes
from jax import lax
from jax.experimental import pallas as pl
from jax.experimental.pallas import tpu as pltpu
from jax.sharding import PartitionSpec as P

GROUP_CH = 256
SPAN = 512
WIDTH = 512
NCTX = 8
OWN = WIDTH // NCTX
BATCHES = ((0, 32), (32, 32))
HALF = SPAN // 2
CHUNKS = ((0, 128), (128, 128), (256, 256))
EARLY = 384
BF = jnp.bfloat16
F32 = jnp.float32
MESH = pl.DeviceIdType.MESH


def tables():
    freq = np.concatenate([np.arange(0, SPAN, 2), np.arange(1, SPAN, 2)])
    angle = np.pi * ((np.arange(SPAN)[:, None] * (2 * freq + 1)[None, :]) % (4 * SPAN)) / (2 * SPAN)
    forward = np.concatenate([np.cos(angle), -np.sin(angle)], axis=1)
    high = forward.astype(ml_dtypes.bfloat16)
    low = (forward - high.astype(np.float64)).astype(ml_dtypes.bfloat16)
    scale = ml_dtypes.bfloat16(1.0 / SPAN)
    return (
        np.stack([high, low]),
        np.stack([np.ascontiguousarray(high.T) * scale, np.ascontiguousarray(low.T) * scale]),
    )


def nt(lhs, rhs):
    return lax.dot_general(lhs, rhs, (((1,), (1,)), ((), ())), preferred_element_type=F32)


def mm(lhs, rhs):
    return jnp.dot(lhs, rhs, preferred_element_type=F32)


def kernel(
    lens_hbm, sw_hbm, skip_hbm, feat, filt, weight, fwd_hbm, inv_hbm,
    out,
    lens, sw, skip, ext, edge, halo, ftmp, fsend, frecv, sbf, ssend, srecv, qbuf, sbuf, fwd, inv, eye,
    spec_h, spec_x, spec_y, yhi, ylo, csend0, csend1, csend2, crecv0, crecv1, crecv2, gbuf, wbuf,
    za1, za1r, za2, za2r, zax, zaxr, zb1, zb1r, zb2, zb2r, zbx, zbxr,
    xa, xar, xa1, xa1r, xa2, xa2r, xb, xbr, xb1, xb1r, xb2, xb2r, keep_a, keep_b, keep_c, keep_d,
    loc, wloc, hs, hr, fs, fr, ss, sr, ws, wr, cs, cr, gs, gr,
    xs, xr, z1s, z1r, z2s, z2r, zxs, zxr, s1s, s1r, s2s, s2r,
):
    c, g = lax.axis_index("ctx"), lax.axis_index("grp")
    z, xh, core = g // 4, (g // 2) % 2, g % 2
    partner = (c, g + 1 - 2 * core)
    across = (c, g + 2 - 4 * xh)
    up = (c, ((z + 1) % 4) * 4 + xh * 2 + core)
    down = (c, ((z + 3) % 4) * 4 + xh * 2 + core)

    def remote(src, dst, send, recv, device):
        return pltpu.make_async_remote_copy(
            src_ref=src, dst_ref=dst, send_sem=send, recv_sem=recv, device_id=device, device_id_type=MESH
        )

    sent = []

    def start(*args):
        copy = remote(*args)
        copy.start()
        sent.append(copy)
        return copy

    def drain(copies):
        for copy in copies:
            copy.wait_send()
        copies.clear()

    def arrived(dst, recv):
        remote(dst, dst, hs.at[0], recv, partner).wait_recv()

    def rows64(ref, index):
        return ref.at[pl.ds(pl.multiple_of(index * OWN, OWN), OWN)]

    def rows16(ref, base, size):
        return ref.at[pl.ds(pl.multiple_of(base, 16), size)]

    barrier = pltpu.get_barrier_semaphore()
    peers = [(lax.rem(c + k, NCTX), g) for k in range(1, NCTX)]
    for device in peers + [partner, across, up, down]:
        pl.semaphore_signal(barrier, inc=1, device_id=device, device_id_type=MESH)

    get_filt = pltpu.make_async_copy(filt, ftmp, loc.at[0])
    get_feat = pltpu.make_async_copy(feat, ext.at[:, pl.ds(16, SPAN)], loc.at[1])
    get_fwd = pltpu.make_async_copy(fwd_hbm, fwd, loc.at[2])
    get_inv = pltpu.make_async_copy(inv_hbm, inv, loc.at[3])
    get_lens = pltpu.make_async_copy(lens_hbm, lens, loc.at[4])
    get_sw = pltpu.make_async_copy(sw_hbm, sw, loc.at[5])
    get_skip = pltpu.make_async_copy(skip_hbm, skip, loc.at[6])
    get_lens.start()
    get_filt.start()
    get_feat.start()
    get_sw.start()
    get_skip.start()
    get_fwd.start()
    get_inv.start()
    mine = pl.ds(pl.multiple_of(core * WIDTH, WIDTH), WIDTH)

    eye[...] = (
        lax.broadcasted_iota(jnp.int32, (HALF, HALF), 0) == lax.broadcasted_iota(jnp.int32, (HALF, HALF), 1)
    ).astype(F32).astype(BF)
    get_lens.wait()
    get_filt.wait()
    for part in range(WIDTH // GROUP_CH):
        length = lens[2 * g + part]
        cols = pl.ds(part * GROUP_CH, GROUP_CH)
        lag = c * SPAN + lax.broadcasted_iota(jnp.int32, (SPAN, GROUP_CH), 0)
        cut = jnp.where(lag < length, ftmp[:, cols].astype(F32), 0.0).astype(BF)
        fsend[cols, :] = nt(eye[...], cut).astype(BF)

    get_feat.wait()
    row = lax.broadcasted_iota(jnp.int32, (16, WIDTH), 0)
    packed = jnp.zeros((16, WIDTH), F32)
    for i in range(3):
        last = pltpu.roll(ext[i, pl.ds(SPAN, 16), :].astype(F32), 2 + 2 * i, 0)
        packed = jnp.where(row // 2 == i, last, packed)
    edge[...] = packed.astype(BF)

    pl.semaphore_wait(barrier, len(peers) + 4)
    start(edge, halo, hs.at[0], hr.at[0], peers[0])
    for k, peer in enumerate(peers):
        start(rows64(fsend, peer[0]), rows64(frecv, c), fs.at[k], fr.at[c], peer)
    own_f = pltpu.make_async_copy(rows64(fsend, c), rows64(frecv, c), fr.at[c])
    own_f.start()


    def short(block):
        base = pl.multiple_of(block * 32, 32)
        here = pl.ds(base, 32)
        res = []
        for i in range(3):
            v = ext[i, pl.ds(base, 48), :].astype(F32)
            acc = sw[0, i : i + 1, :] * v[16:]
            acc = acc + sw[1, i : i + 1, :] * pltpu.roll(v, 1, 0)[16:]
            acc = acc + sw[2, i : i + 1, :] * pltpu.roll(v, 2, 0)[16:]
            res.append(acc)
        qbuf[here, :] = res[0]
        signal = res[1] * res[2]
        sbuf[here, :] = res[0] * (skip[...] * signal)
        sbf[here, :] = signal.astype(BF)

    get_sw.wait()
    get_skip.wait()

    @pl.loop(1, SPAN // 32)
    def _(block):
        short(block)

    arrived(halo, hr.at[0])
    before = jnp.where(lax.broadcast_in_dim(c, (16, WIDTH), ()) > 0, halo[...].astype(F32), 0.0)
    for i in range(3):
        ext[i, pl.ds(0, 16), :] = pltpu.roll(before, 14 - 2 * i, 0).astype(BF)
    short(0)
    for part in range(2):
        cols = pl.ds(part * HALF, HALF)
        ssend[cols, :] = nt(eye[...], sbf[:, cols]).astype(BF)
    def send_signal(b):
        off, size = BATCHES[b]
        for k, peer in enumerate(peers):
            start(
                rows16(ssend, peer[0] * OWN + off, size), rows16(srecv, NCTX * off + c * size, size),
                ss.at[b, k], sr.at[b, c], peer,
            )
        pltpu.make_async_copy(
            rows16(ssend, c * OWN + off, size), rows16(srecv, NCTX * off + c * size, size), sr.at[b, c]
        ).start()

    send_signal(0)
    send_signal(1)

    get_w = []
    for p in range(8):
        keep_cols = pl.ds(pl.multiple_of((2 * p + core) * WIDTH, WIDTH), WIDTH)
        give_cols = pl.ds(pl.multiple_of((2 * p + 1 - core) * WIDTH, WIDTH), WIDTH)
        copy = pltpu.make_async_copy(weight.at[:, keep_cols], wbuf.at[p, mine], wloc.at[p])
        copy.start()
        get_w.append(copy)
        start(weight.at[:, give_cols], wbuf.at[p, mine], ws.at[p], wr.at[p], partner)

    get_fwd.wait()

    def transform(block, spec):
        for n in range(0, 2 * SPAN, HALF):
            cols = pl.ds(n, HALF)
            spec[:, cols] = mm(block[...], fwd[0, :, cols]) + mm(block[...], fwd[1, :, cols])

    for k in range(NCTX):
        arrived(rows64(frecv, k), fr.at[k])
    transform(frecv, spec_h)

    def products(off, size):
        for lane in range(4):
            re, im = pl.ds(lane * 128, 128), pl.ds(SPAN + lane * 128, 128)

            @pl.loop(0, size // 8)
            def _(r, re=re, im=im, odd=lane >= 2):
                def taps(d):
                    return pl.ds(pl.multiple_of(d * OWN + off + r * 8, 8), 8)

                def rows(j):
                    return pl.ds(pl.multiple_of(NCTX * off + j * size + r * 8, 8), 8)

                h_re = [spec_h[taps(d), re] for d in range(NCTX)]
                h_im = [spec_h[taps(d), im] for d in range(NCTX)]
                if odd:
                    g_re = [h_re[0]] + [h_re[d] + h_im[d - 1] for d in range(1, NCTX)]
                    g_im = [h_im[0]] + [h_im[d] - h_re[d - 1] for d in range(1, NCTX)]
                else:
                    g_re = [h_re[0]] + [h_re[d] - h_im[d - 1] for d in range(1, NCTX)]
                    g_im = [h_im[0]] + [h_im[d] + h_re[d - 1] for d in range(1, NCTX)]
                x_re = [spec_x[rows(j), re] for j in range(NCTX)]
                x_im = [spec_x[rows(j), im] for j in range(NCTX)]
                for i in range(NCTX):
                    y_re = x_re[0] * g_re[i] - x_im[0] * g_im[i]
                    y_im = x_re[0] * g_im[i] + x_im[0] * g_re[i]
                    for j in range(1, i + 1):
                        y_re = y_re + x_re[j] * g_re[i - j] - x_im[j] * g_im[i - j]
                        y_im = y_im + x_re[j] * g_im[i - j] + x_im[j] * g_re[i - j]
                    spec_y[rows(i), re] = y_re
                    spec_y[rows(i), im] = y_im

        @pl.loop(0, NCTX * size // 32)
        def _(r):
            rows = pl.ds(pl.multiple_of(NCTX * off + r * 32, 32), 32)
            value = spec_y[rows, :]
            high = value.astype(BF)
            yhi[rows, :] = high
            ylo[rows, :] = (value - high.astype(F32)).astype(BF)

    csend, crecv = (csend0, csend1, csend2), (crecv0, crecv1, crecv2)

    def inverse(t, off, size):
        rows, cols = pl.ds(NCTX * off, NCTX * size), pl.ds(*CHUNKS[t])
        back = mm(yhi[rows, :], inv[0, :, cols]) + mm(ylo[rows, :], inv[0, :, cols]) + mm(yhi[rows, :], inv[1, :, cols])
        for i in range(NCTX):
            csend[t][pl.ds(i * OWN + off, size), :] = back[i * size : (i + 1) * size].astype(BF)

    def give_back(t, b, off, size):
        for k, peer in enumerate(peers):
            start(
                rows16(csend[t], peer[0] * OWN + off, size), rows16(crecv[t], c * OWN + off, size),
                cs.at[t, b, k], cr.at[t, b, c], peer,
            )
        pltpu.make_async_copy(
            rows16(csend[t], c * OWN + off, size), rows16(crecv[t], c * OWN + off, size), cr.at[t, b, c]
        ).start()

    get_inv.wait()
    for b, (off, size) in enumerate(BATCHES):
        for k in range(NCTX):
            arrived(rows16(srecv, NCTX * off + k * size, size), sr.at[b, k])
        batch = pl.ds(NCTX * off, NCTX * size)
        transform(srecv.at[batch], spec_x.at[batch])
        products(off, size)
        inverse(0, off, size)
        give_back(0, b, off, size)
    for t in range(1, len(CHUNKS)):
        inverse(t, 0, BATCHES[0][1])
        for off, size in BATCHES[1:]:
            inverse(t, off, size)
        give_back(t, 0, 0, OWN)

    def gate(t):
        for b, (off, size) in enumerate(BATCHES if t == 0 else ((0, OWN),)):
            for k in range(NCTX):
                arrived(rows16(crecv[t], k * OWN + off, size), cr.at[t, b, k])
        rows = pl.ds(*CHUNKS[t])
        conv = nt(eye[: CHUNKS[t][1], : CHUNKS[t][1]], crecv[t][...])
        gated = qbuf[rows, :] * conv + sbuf[rows, :]
        gbuf[core, rows] = gated.astype(BF)
        start(gbuf.at[core, rows], gbuf.at[core, rows], gs.at[t], gr.at[t], partner)

    def met(t):
        arrived(gbuf.at[1 - core, pl.ds(*CHUNKS[t])], gr.at[t])

    def place(dz, other):
        return ((z + dz) % 4) * 2 + (1 - xh if other else xh)

    def project(t, dz, other, cols):
        p, rows = place(dz, other), pl.ds(*CHUNKS[t])
        return mm(gbuf[0, rows], wbuf[p, :WIDTH, cols]) + mm(gbuf[1, rows], wbuf[p, WIDTH:, cols])

    every, early, late = slice(0, WIDTH), slice(0, EARLY), slice(EARLY, WIDTH)
    z_parts = (
        (0, every, za1, za1r, za2, za2r, zax, zaxr, keep_a),
        (2, early, zb1, zb1r, zb2, zb2r, zbx, zbxr, keep_b),
    )
    x_parts = (
        (1, every, xa, xar, xa1, xa1r, xa2, xa2r, keep_c),
        (2, late, xb, xbr, xb1, xb1r, xb2, xb2r, keep_d),
    )

    def halves(t):
        size = CHUNKS[t][1] // 2
        return pl.ds(0, size), pl.ds(size, size)

    def first(q, o, value):
        t, _, send, recv, *_ = z_parts[q]
        top, low = halves(t)
        send[o] = value.astype(BF)
        start(send.at[o, top], recv.at[0, o], z1s.at[q, 0, o], z1r.at[q, 0, o], up)
        start(send.at[o, low], recv.at[1, o], z1s.at[q, 1, o], z1r.at[q, 1, o], down)

    def second(q, o):
        t, cols, _, had, send, recv, _, _, keep = z_parts[q]
        top, low = halves(t)
        for d, dz, rows, device in ((0, 1, top, up), (1, 3, low, down)):
            keep[...] = project(t, dz, o, cols)
            arrived(had.at[d, o], z1r.at[q, d, o])
            keep[rows, :] += had[d, o].astype(F32)
            send[d, o] = keep[...].astype(BF)
            start(send.at[d, o], recv.at[d, o], z2s.at[q, d, o], z2r.at[q, d, o], device)

    def third(q):
        t, cols, _, _, _, had, send, recv, keep = z_parts[q]
        keep[...] = project(t, 0, 1, cols)
        for d in range(2):
            arrived(had.at[d, 1], z2r.at[q, d, 1])
        send[...] = (keep[...] + had[0, 1].astype(F32) + had[1, 1].astype(F32)).astype(BF)
        start(send, recv, zxs.at[q], zxr.at[q], across)

    def last(q):
        t, cols, _, _, _, had, _, recv, keep = z_parts[q]
        for d in range(2):
            arrived(had.at[d, 0], z2r.at[q, d, 0])
        arrived(recv, zxr.at[q])
        total = keep[...] + had[0, 0].astype(F32) + had[1, 0].astype(F32) + recv[...].astype(F32)
        out[pl.ds(*CHUNKS[t]), cols] = total.astype(BF)

    def over_x(q, dz):
        t, cols, send, recv, *_ = x_parts[q]
        send[dz] = project(t, dz, 1, cols).astype(BF)
        start(send.at[dz], recv.at[dz], xs.at[q, dz], xr.at[q, dz], across)

    def summed(q, dz):
        t, cols, _, had, *_, keep = x_parts[q]
        keep[...] = project(t, dz, 0, cols)
        arrived(had.at[dz], xr.at[q, dz])
        keep[...] += had[dz].astype(F32)

    def apart(q):
        t, _, _, _, send, recv, _, _, keep = x_parts[q]
        top, low = halves(t)
        summed(q, 2)
        send[...] = keep[...].astype(BF)
        start(send.at[top], recv.at[0], s1s.at[q, 0], s1r.at[q, 0], up)
        start(send.at[low], recv.at[1], s1s.at[q, 1], s1r.at[q, 1], down)

    def forward(q):
        t, _, _, _, _, had, send, recv, keep = x_parts[q]
        top, low = halves(t)
        for d, dz, rows, device in ((0, 1, top, up), (1, 3, low, down)):
            summed(q, dz)
            arrived(had.at[d], s1r.at[q, d])
            keep[rows, :] += had[d].astype(F32)
            send[d] = keep[...].astype(BF)
            start(send.at[d], recv.at[d], s2s.at[q, d], s2r.at[q, d], device)

    def close(q):
        t, cols, _, _, _, _, _, had, keep = x_parts[q]
        for d in range(2):
            arrived(had.at[d], s2r.at[q, d])
        out[pl.ds(*CHUNKS[t]), cols] = (keep[...] + had[0].astype(F32) + had[1].astype(F32)).astype(BF)

    for p in range(8):
        get_w[p].wait()
        arrived(wbuf.at[p, pl.ds(pl.multiple_of((1 - core) * WIDTH, WIDTH), WIDTH)], wr.at[p])
    gate(0)
    before = sent[:]
    sent.clear()
    other, rows = pl.ds(pl.multiple_of((1 - core) * WIDTH, WIDTH), WIDTH), pl.ds(*CHUNKS[0])
    for o, keep in ((1, keep_a), (0, keep_c)):
        keep[...] = mm(gbuf[core, rows], wbuf[place(2, o), mine, :])
    met(0)
    for o, keep in ((1, keep_a), (0, keep_c)):
        first(0, o, keep[...] + mm(gbuf[1 - core, rows], wbuf[place(2, o), other, :]))
    gate(1)
    met(1)
    for dz in (2, 1, 3):
        over_x(0, dz)
    second(0, 1)
    gate(2)
    met(2)
    for o in (1, 0):
        first(1, o, project(2, 2, o, early))
    for dz in (2, 1, 3):
        over_x(1, dz)
    over_x(0, 0)
    over_x(1, 0)
    apart(0)
    third(0)
    second(1, 1)
    drain(before)
    apart(1)
    second(0, 0)
    forward(0)
    before = sent[:-6]
    del sent[:-6]
    second(1, 0)
    third(1)
    forward(1)
    for t, cols, *_, keep in z_parts:
        keep[...] = project(t, 0, 0, cols)
    for q in range(2):
        summed(q, 0)
    drain(before)
    last(0)
    close(0)
    last(1)
    close(1)
    drain(sent)


def per_device(features, short_weight, long_filter, lengths, skip_gain, out_weight):
    forward, inverse = tables()
    dma = pltpu.SemaphoreType.DMA
    vm = pltpu.VMEM
    sizes = [size for _, size in CHUNKS]
    z_shapes = ((sizes[0], WIDTH), (sizes[2], EARLY))
    x_shapes = ((sizes[1], WIDTH), (sizes[2], WIDTH - EARLY))
    scratch = [
        pltpu.SMEM((32,), jnp.int32), vm((3, 3, WIDTH), F32), vm((1, WIDTH), F32),
        vm((3, 16 + SPAN, WIDTH), BF), vm((16, WIDTH), BF), vm((16, WIDTH), BF),
        vm((SPAN, WIDTH), BF), vm((WIDTH, SPAN), BF), vm((WIDTH, SPAN), BF),
        vm((SPAN, WIDTH), BF), vm((WIDTH, SPAN), BF), vm((WIDTH, SPAN), BF),
        vm((SPAN, WIDTH), F32), vm((SPAN, WIDTH), F32),
        vm((2, SPAN, 2 * SPAN), BF), vm((2, 2 * SPAN, SPAN), BF), vm((HALF, HALF), BF),
        vm((WIDTH, 2 * SPAN), F32), vm((WIDTH, 2 * SPAN), F32), vm((WIDTH, 2 * SPAN), F32),
        vm((WIDTH, 2 * SPAN), BF), vm((WIDTH, 2 * SPAN), BF),
        *[vm((WIDTH, size), BF) for size in sizes], *[vm((WIDTH, size), BF) for size in sizes],
        vm((2, SPAN, WIDTH), BF), vm((8, 2 * WIDTH, WIDTH), BF),
    ]
    for rows, cols in z_shapes:
        scratch += [
            vm((2, rows, cols), BF), vm((2, 2, rows // 2, cols), BF),
            vm((2, 2, rows, cols), BF), vm((2, 2, rows, cols), BF),
            vm((rows, cols), BF), vm((rows, cols), BF),
        ]
    for rows, cols in x_shapes:
        scratch += [
            vm((4, rows, cols), BF), vm((4, rows, cols), BF),
            vm((rows, cols), BF), vm((2, rows // 2, cols), BF),
            vm((2, rows, cols), BF), vm((2, rows, cols), BF),
        ]
    scratch += [
        *[vm(shape, F32) for shape in z_shapes + x_shapes],
        dma((7,)), dma((8,)), dma((1,)), dma((1,)),
        dma((7,)), dma((8,)), dma((2, 7)), dma((2, 8)), dma((8,)), dma((8,)),
        dma((3, 2, 7)), dma((3, 2, 8)), dma((3,)), dma((3,)),
        dma((2, 4)), dma((2, 4)), dma((2, 2, 2)), dma((2, 2, 2)), dma((2, 2, 2)), dma((2, 2, 2)),
        dma((2,)), dma((2,)), dma((2, 2)), dma((2, 2)), dma((2, 2)), dma((2, 2)),
    ]
    hbm = pl.BlockSpec(memory_space=pl.ANY)
    near = pl.BlockSpec(memory_space=pltpu.VMEM)
    return pl.pallas_call(
        kernel,
        out_shape=pltpu.VMEM((SPAN, WIDTH), BF),
        in_specs=[hbm] * 8,
        out_specs=near,
        scratch_shapes=scratch,
        name="hyena",
        compiler_params=pltpu.CompilerParams(
            collective_id=0, has_side_effects=True, vmem_limit_bytes=56 * 2**20
        ),
    )(
        lengths, short_weight, skip_gain.reshape(1, WIDTH), features, long_filter, out_weight,
        jnp.asarray(forward), jnp.asarray(inverse),
    )


def solution(mesh):
    return jax.shard_map(
        per_device,
        mesh=mesh,
        in_specs=(
            P(None, "ctx", "grp"),
            P(None, None, "grp"),
            P("ctx", "grp"),
            P(),
            P("grp"),
            P("grp", None),
        ),
        out_specs=P("ctx", "grp"),
        check_vma=False,
    )
```
